128 devices in a mesh: dp: 8 (over y_hi, z), fsdp: 16 (over y_lo, x, core).
Axes of the slice: x: 4, y: 4 (y_hi: 2, y_lo: 2; y = y_hi * 2 + y_lo), z: 4, core: 2. Of those that a mesh axis runs over, the one named last changes fastest.
Arguments:
- rollout_rows: bfloat16 [1024, 32, 8192], P(('dp', 'fsdp')), may hold values from -6 to 6
- rewards: float32 [1024], P(('dp', 'fsdp')), may hold values from -5 to 5
- group_ids: int32 [1024], P(('dp', 'fsdp')), may hold values from 0 to 63
- lengths: int32 [1024], P(('dp', 'fsdp')), may hold values from 1 to 32, 28672 in all
- packing: int32 [1024], P(('dp', 'fsdp')), may hold values from 0 to 1023, as said below
- queries: bfloat16 [32768, 4096], P(('dp', 'fsdp'))
- keys: bfloat16 [32768, 512], P(('dp', 'fsdp')), may hold values from -6 to 6
- out_grad: bfloat16 [32768, 4096], P(('dp', 'fsdp')), may hold values from -6 to 6
- value_weight: bfloat16 [8192, 512], P('fsdp'), may hold values from -0.0625 to 0.0625
Outputs:
- attn_out: bfloat16 [32768, 4096], P(('dp', 'fsdp'))
- grad_rows: bfloat16 [32768, 8192], P(('dp', 'fsdp'))
- grad_weight: bfloat16 [8, 8192, 512], P('dp', 'fsdp')
The draws below stay inside these ranges and needn't reach their ends.
Inputs may be any that keep to these rules, and one draw needn't show every extreme that they name: packing is a bijection onto 0 to 1023. Rollout row b * 8 + s (b = device block in dp+fsdp order) goes to a trainer slot of a block b' with the same fsdp index. From one device at most 2 rollouts go to any one device, and exactly 2 to some device; among devices of one fsdp index, the number of rollouts sent from dp index p to dp index (p + o) mod 8 depends on o only; each device receives exactly 8. `group_ids`: some groups may be empty.
All inputs are finite; a program needn't handle non-finite values. No bound on the sum of `lengths` on one device may be relied on, other than what follows from the above.
Results may differ from the reference program's by a relative error of at most 0.023.
Values may be sent and summed in bfloat16 or wider, within the bound.
No kernel may reach another device: no remote copies, remote signals or barrier semaphores. Data moves between devices by JAX's collectives and lax.ppermute only.
A program may use at most 128 MiB of HBM per device.

```python
import math
import jax
import jax.numpy as jnp
import numpy as np
from jax import lax

D = 8192
HD = 128
KVH = 4
QH = 32
L = 32
SLOTS = 8
DV = 512
DQ = 4096
ROLL = 1024
GROUPS = 64
TOKENS = 32768
N_DP = 8
N_FSDP = 16


def column_offsets(col_key):
    capacity = 2 * SLOTS // N_DP
    first_key, pool_key = jax.random.split(col_key)
    order = jax.random.permutation(first_key, jnp.arange(N_DP, dtype=jnp.int32))
    pool = jnp.repeat(order[1:], capacity)
    chosen = jax.random.permutation(pool_key, pool)[:SLOTS - capacity]
    leading = jnp.zeros((capacity,), jnp.int32) + order[0]
    return jnp.concatenate([leading, chosen])


def draw_packing(key, part):
    key = jax.random.fold_in(key, 11)
    key_shift, key_source, key_target = jax.random.split(key, 3)
    shift_keys = jax.random.split(key_shift, N_FSDP)
    offsets = jax.vmap(column_offsets)(shift_keys)
    source_keys = jax.random.split(key_source, N_DP * N_FSDP)
    target_keys = jax.random.split(key_target, N_DP * N_FSDP)
    base = jnp.arange(SLOTS, dtype=jnp.int32)
    source_order = jax.vmap(lambda sub_key: jax.random.permutation(sub_key, base))(source_keys).reshape(N_DP, N_FSDP, SLOTS)
    target_order = jax.vmap(lambda sub_key: jax.random.permutation(sub_key, base))(target_keys).reshape(N_DP, N_FSDP, SLOTS)
    src = jnp.arange(N_DP, dtype=jnp.int32)[:, None, None]
    column = jnp.arange(N_FSDP, dtype=jnp.int32)[None, :, None]
    ordinal = jnp.arange(SLOTS, dtype=jnp.int32)[None, None, :]
    src_full = jnp.broadcast_to(src, (N_DP, N_FSDP, SLOTS))
    column_full = jnp.broadcast_to(column, (N_DP, N_FSDP, SLOTS))
    ordinal_full = jnp.broadcast_to(ordinal, (N_DP, N_FSDP, SLOTS))
    dest = (src_full + offsets[column_full, ordinal_full]) % N_DP
    target_slot = target_order[dest, column_full, ordinal_full]
    source_slot = source_order[src_full, column_full, ordinal_full]
    value = (dest * N_FSDP + column_full) * SLOTS + target_slot
    table = jnp.zeros((N_DP, N_FSDP, SLOTS), jnp.int32).at[src_full, column_full, source_slot].set(value)
    return table.reshape(ROLL)


def draw_queries(key, part):
    key = jax.random.fold_in(key, 5)
    key_base = jax.random.fold_in(key, 0)
    return jax.random.normal(key_base, (TOKENS, QH * HD), jnp.float32).astype(jnp.bfloat16)


def set_ends(entries, stream_key, smallest, high):
    place = [jax.random.randint(jax.random.fold_in(stream_key, axis), (), 0, length) for axis, length in enumerate(entries.shape)]
    longest = entries.shape.index(max(entries.shape))
    beside = place[:longest] + [(place[longest] + 1) % entries.shape[longest]] + place[longest + 1:]
    return entries.at[tuple(place)].set(smallest).at[tuple(beside)].set(high)


def block_scale(stream_key, dims, shards, low, high):
    factor_of = 1.0
    for dim, blocks in shards:
        draws = jax.random.uniform(jax.random.fold_in(jax.random.fold_in(stream_key, 6), dim), (blocks,), jnp.float32, low / len(shards), high / len(shards))
        factor_of = factor_of * jnp.repeat(jnp.exp(draws), dims[dim] // blocks).reshape((-1,) + (1,) * (len(dims) - 1 - dim))
    return factor_of


def split_up(number_of, total, reach, slope):
    weights = [(1 << 20) // math.isqrt(standing ** slope) + 1 for standing in range(2, number_of + 1)]
    spare, given = total - reach - (number_of - 1), [1] * (number_of - 1)
    while spare > 0:
        movable = [i for i in range(number_of - 1) if given[i] < reach]
        whole, left = sum([weights[i] for i in movable]), spare
        for i in movable:
            extra = min(reach - given[i], max(1, left * weights[i] // whole), spare)
            given[i] = given[i] + extra
            spare = spare - extra
    return np.array([reach] + given)


def ragged(own_key, number_of, total, limit, slope):
    if number_of == 2:
        one = jax.random.randint(own_key, (), max(1, total - limit), min(limit, total - 1) + 1)
        return jnp.stack([one, total - one])
    sizes = jnp.asarray(split_up(number_of, total, limit, slope), jnp.int32)
    twos = (number_of - 1) // 2
    giver, receiver = sizes[1:1 + 2 * twos:2], sizes[2:2 + 2 * twos:2]
    room = jnp.minimum(giver - 1, limit - receiver)
    shifted = jax.random.randint(jax.random.fold_in(own_key, 1), (twos,), 0, 1 << 20) % (room + 1)
    sizes = sizes.at[1:1 + 2 * twos:2].set(giver - shifted).at[2:2 + 2 * twos:2].set(receiver + shifted)
    return sizes[jax.random.permutation(jax.random.fold_in(own_key, 2), number_of)]


def gaussian(rng, extent, spread, limit, shards=(), kind=jnp.bfloat16):
    result = jax.random.normal(rng, extent, jnp.float32) * spread
    if len(shards) > 0:
        result = block_scale(rng, extent, shards, -0.22, 0.18) * result
    return jnp.clip(result, min=-limit, max=limit).astype(kind)


def setup_inputs(seed: int = 0) -> dict:
    splits = jax.random.split(jax.random.key(seed), 10)
    rollout_rows = gaussian(splits[0], (ROLL, L, D), 1.0, 6.0, ((0, 128),))
    rewards = gaussian(splits[1], (ROLL,), 1.0, 5.0, ((0, 128),), jnp.float32)
    group_ids = set_ends(jax.random.randint(splits[2], (ROLL,), 0, GROUPS), jax.random.fold_in(splits[2], 1), 0, GROUPS - 1).astype(jnp.int32)
    lengths = ragged(splits[3], ROLL, ROLL * 7 * L // 8, L, 1).astype(jnp.int32)
    packing = draw_packing(jax.random.fold_in(splits[9], 71), 0)
    queries = draw_queries(jax.random.fold_in(splits[9], 71), 0)
    keys = gaussian(splits[6], (TOKENS, DV), 1.0, 6.0, ((0, 128),))
    out_grad = gaussian(splits[7], (TOKENS, DQ), 1.0, 6.0, ((0, 128),))
    value_weight = gaussian(splits[8], (D, DV), D ** -0.5, 0.0625, ((0, 16),))
    return {"rollout_rows": rollout_rows, "rewards": rewards, "group_ids": group_ids, "lengths": lengths, "packing": packing, "queries": queries, "keys": keys, "out_grad": out_grad, "value_weight": value_weight}


def reference(rollout_rows, rewards, group_ids, lengths, packing, queries, keys, out_grad, value_weight):
    group_hit = (group_ids[:, None] == jnp.arange(GROUPS, dtype=jnp.int32)[None, :]).astype(jnp.float32)
    totals = lax.optimization_barrier(jnp.sum(group_hit * rewards[:, None], axis=0))
    counts = lax.optimization_barrier(jnp.sum(group_hit, axis=0))
    means = totals / jnp.maximum(counts, 1.0)
    advantage = (rewards - means[group_ids]).astype(jnp.bfloat16)
    packed_rows = jnp.zeros((ROLL, L, D), jnp.bfloat16).at[packing].set(rollout_rows)
    packed_len = jnp.zeros((ROLL,), jnp.int32).at[packing].set(lengths)
    packed_adv = jnp.zeros((ROLL,), jnp.bfloat16).at[packing].set(advantage)
    flat_rows = packed_rows.reshape(TOKENS, D)
    values = jnp.dot(flat_rows, value_weight, preferred_element_type=jnp.float32).astype(jnp.bfloat16)
    group_q = QH // KVH
    query_heads = queries.reshape(ROLL, L, KVH, group_q, HD).astype(jnp.float32)
    key_heads = keys.reshape(ROLL, L, KVH, HD).astype(jnp.float32)
    value_heads = values.reshape(ROLL, L, KVH, HD).astype(jnp.float32)
    scores = jnp.einsum('sikgd,sjkd->skgij', query_heads, key_heads) / jnp.sqrt(jnp.float32(HD))
    position = jnp.arange(L, dtype=jnp.int32)
    live = position[None, :] < packed_len[:, None]
    causal = position[:, None] >= position[None, :]
    allowed = causal[None, None, None, :, :] & live[:, None, None, None, :]
    masked = jnp.where(allowed, scores, -jnp.inf)
    top = lax.optimization_barrier(jnp.max(masked, axis=-1, keepdims=True))
    weights = jnp.where(allowed, jnp.exp(masked - top), 0.0)
    probs = (weights / lax.optimization_barrier(jnp.sum(weights, axis=-1, keepdims=True))).astype(jnp.bfloat16)
    outputs = jnp.einsum('skgij,sjkd->sikgd', probs.astype(jnp.float32), value_heads)
    query_live = live.astype(jnp.float32)[:, :, None, None, None]
    attn_out = (outputs * query_live).astype(jnp.bfloat16).reshape(TOKENS, QH * HD)
    factor = -packed_adv.astype(jnp.float32) * L / packed_len.astype(jnp.float32)
    cot = (factor[:, None, None, None, None] * query_live * out_grad.reshape(ROLL, L, KVH, group_q, HD).astype(jnp.float32)).astype(jnp.bfloat16)
    dvalues = jnp.einsum('skgij,sikgd->sjkd', probs.astype(jnp.float32), cot.astype(jnp.float32)).astype(jnp.bfloat16)
    dvalues = dvalues.reshape(TOKENS, KVH * HD)
    grad_rows = lax.dot_general(dvalues, value_weight, (((1,), (1,)), ((), ())), preferred_element_type=jnp.float32).astype(jnp.bfloat16)
    row_blocks = flat_rows.reshape(N_DP, N_FSDP, SLOTS * L, D)
    grad_blocks = dvalues.reshape(N_DP, N_FSDP, SLOTS * L, KVH * HD)

    def shard_grad(pair):
        block_rows, block_grads = pair

        def add_one(total, item):
            partial_sum = lax.dot_general(item[0], item[1], (((0,), (0,)), ((), ())), preferred_element_type=jnp.float32)
            rounded = lax.optimization_barrier(partial_sum.astype(jnp.bfloat16))
            return (total + rounded.astype(jnp.float32), None)
        start = jnp.zeros((D, KVH * HD), jnp.float32)
        total, unused = lax.scan(add_one, start, (block_rows, block_grads))
        return (total / N_FSDP).astype(jnp.bfloat16)
    grad_weight = lax.map(shard_grad, (row_blocks, grad_blocks))
    return (attn_out, grad_rows, grad_weight)
```

```python
import functools

import jax
import jax.numpy as jnp
from jax import lax
from jax.experimental import pallas as pl
from jax.experimental.pallas import tpu as pltpu
from jax.sharding import PartitionSpec as P

HD = 128
VMEM = 56 * 1024 * 1024


def params(**kw):
    return pltpu.CompilerParams(vmem_limit_bytes=VMEM, **kw)


def prepare_body(slots, dp, fsdp, where, packing, lengths, rewards, groups, info, order):
    lane = lax.broadcasted_iota(jnp.int32, info.shape, 1)
    told = jnp.zeros(info.shape, jnp.float32)
    for r in range(slots):
        told = jnp.where(lane == r, packing[r].astype(jnp.float32), told)
        told = jnp.where(lane == slots + r, lengths[r].astype(jnp.float32), told)
        told = jnp.where(lane == 2 * slots + r, rewards[r], told)
        told = jnp.where(lane == 3 * slots + r, groups[r].astype(jnp.float32), told)
    info[...] = told
    home = where[1]
    offsets = [lax.rem(lax.div(packing[r], slots * fsdp) - home + dp, dp) for r in range(slots)]
    mine = jnp.int32(0)
    for r in range(slots):
        colour = jnp.int32(0)
        for k in range(slots):
            if k != r:
                first = offsets[k] <= offsets[r] if k < r else offsets[k] < offsets[r]
                colour = colour + jnp.where(first, 1, 0)
        order[r] = colour
        mine = mine + jnp.where(colour == home, offsets[r], 0)
    order[slots] = mine


def prepare(where, packing, lengths, rewards, groups, dp, fsdp):
    slots = packing.shape[0]
    smem = pl.BlockSpec(memory_space=pltpu.SMEM)
    return pl.pallas_call(
        functools.partial(prepare_body, slots, dp, fsdp),
        in_specs=[smem] * 5,
        out_specs=[pl.BlockSpec(memory_space=pltpu.VMEM), smem],
        out_shape=[
            jax.ShapeDtypeStruct((dp * fsdp, 4 * slots), jnp.float32),
            jax.ShapeDtypeStruct((slots + 1,), jnp.int32),
        ],
        name="prepare",
    )(where, packing, lengths, rewards, groups)


def pack_body(fsdp, order, rows, out, held, cut, arrive, leave):
    slots, _, width = rows.shape
    part = width // fsdp
    ins = [pltpu.make_async_copy(rows.at[r], held.at[r], arrive.at[r]) for r in range(slots)]
    outs = [pltpu.make_async_copy(cut.at[r], out.at[order[r]], leave.at[r]) for r in range(slots)]
    for copy in ins:
        copy.start()
    for r in range(slots):
        ins[r].wait()
        for f in range(fsdp):
            cut[r, f] = held[r, :, f * part : (f + 1) * part]
        outs[r].start()
    for copy in outs:
        copy.wait()


def pack(order, rows, fsdp):
    slots, seq, width = rows.shape
    part = width // fsdp
    return pl.pallas_call(
        functools.partial(pack_body, fsdp),
        in_specs=[pl.BlockSpec(memory_space=pltpu.SMEM), pl.BlockSpec(memory_space=pl.ANY)],
        out_specs=pl.BlockSpec(memory_space=pl.ANY),
        out_shape=jax.ShapeDtypeStruct((slots, fsdp, seq, part), rows.dtype),
        scratch_shapes=[
            pltpu.VMEM((slots, seq, width), rows.dtype),
            pltpu.VMEM((slots, fsdp, seq, part), rows.dtype),
            pltpu.SemaphoreType.DMA((slots,)),
            pltpu.SemaphoreType.DMA((slots,)),
        ],
        compiler_params=params(),
        cost_estimate=pl.CostEstimate(
            flops=0, bytes_accessed=2 * rows.size * 2, transcendentals=0
        ),
        name="pack_rows",
    )(order, rows)


def turn_body(dp, slots, order, rows, out, held, arrive, leave):
    ins = [pltpu.make_async_copy(rows.at[p], held.at[p], arrive.at[p]) for p in range(dp)]
    outs = []
    for p in range(dp):
        dest = lax.rem(order[slots] + p, dp)
        outs.append(pltpu.make_async_copy(held.at[p], out.at[dest], leave.at[p]))
    for copy in ins:
        copy.start()
    for p in range(dp):
        ins[p].wait()
        outs[p].start()
    for copy in outs:
        copy.wait()


def turn(order, rows):
    dp = rows.shape[0]
    return pl.pallas_call(
        functools.partial(turn_body, dp, order.shape[0] - 1),
        in_specs=[pl.BlockSpec(memory_space=pltpu.SMEM), pl.BlockSpec(memory_space=pl.ANY)],
        out_specs=pl.BlockSpec(memory_space=pl.ANY),
        out_shape=jax.ShapeDtypeStruct(rows.shape, rows.dtype),
        scratch_shapes=[
            pltpu.VMEM(rows.shape, rows.dtype),
            pltpu.SemaphoreType.DMA((dp,)),
            pltpu.SemaphoreType.DMA((dp,)),
        ],
        compiler_params=params(),
        cost_estimate=pl.CostEstimate(
            flops=0, bytes_accessed=2 * rows.size * 2, transcendentals=0
        ),
        name="turn_rows",
    )(order, rows)


def plan_body(slots, dp, fsdp, seq, me, info, length, colours, factor):
    packing = info[0:slots, :]
    lengths = info[slots : 2 * slots, :]
    rewards = info[2 * slots : 3 * slots, :]
    groups = info[3 * slots : 4 * slots, :]
    lane = lax.broadcasted_iota(jnp.int32, packing.shape, 1)
    row = lax.broadcasted_iota(jnp.int32, packing.shape, 0)
    target = lax.div(packing.astype(jnp.int32), slots * fsdp)

    offset = lax.rem(target - lax.div(lane, fsdp) + dp, dp)
    colour = jnp.zeros(packing.shape, jnp.int32)
    for k in range(1, slots):
        other = pltpu.roll(offset, k, 0)
        first = (other < offset) | ((other == offset) & (row >= k))
        colour = colour + jnp.where(first, 1, 0)
    colour = colour.astype(jnp.float32)

    def total(x):
        return jnp.sum(jnp.sum(x, axis=0, keepdims=True), axis=1, keepdims=True)

    for s in range(slots):
        hit = jnp.where(packing == (me[0] * slots + s).astype(jnp.float32), 1.0, 0.0)
        size = total(hit * lengths)
        reward = total(hit * rewards)
        same = jnp.where(groups == total(hit * groups), 1.0, 0.0)
        mean = total(same * rewards) / jnp.maximum(total(same), 1.0)
        advantage = (reward - mean).astype(jnp.bfloat16).astype(jnp.float32)
        factor[s : s + 1, :] = jnp.broadcast_to(-advantage * seq / size, (1, 128))
        colours[s] = total(hit * colour)[0, 0].astype(jnp.int32)
        length[s] = size[0, 0].astype(jnp.int32)


def plan(me, info, slots, dp, fsdp, seq):
    smem = pl.BlockSpec(memory_space=pltpu.SMEM)
    vmem = pl.BlockSpec(memory_space=pltpu.VMEM)
    return pl.pallas_call(
        functools.partial(plan_body, slots, dp, fsdp, seq),
        in_specs=[smem, vmem],
        out_specs=[smem, smem, vmem],
        out_shape=[
            jax.ShapeDtypeStruct((slots,), jnp.int32),
            jax.ShapeDtypeStruct((slots,), jnp.int32),
            jax.ShapeDtypeStruct((slots, 128), jnp.float32),
        ],
        cost_estimate=pl.CostEstimate(flops=1, bytes_accessed=1, transcendentals=0),
        name="plan_slots",
    )(me, info)


def stack_heads(ref, kh, group):
    cols = [ref[:, (kh * group + g) * HD : (kh * group + g + 1) * HD] for g in range(group)]
    return jnp.concatenate(cols, axis=0)


def probs_body(kv, group, slots, length, colours, factor, q, k, og, dv, turned, probs, held):
    s = pl.program_id(0)
    seq = q.shape[0]
    size = length[s]
    scale = factor[pl.ds(s, 1), :]
    key_pos = lax.broadcasted_iota(jnp.int32, (seq, group * seq), 0)
    query_pos = lax.rem(lax.broadcasted_iota(jnp.int32, (seq, group * seq), 1), seq)
    allowed = (key_pos <= query_pos) & (key_pos < size)
    live = query_pos < size
    shares = []
    for kh in range(kv):
        queries = stack_heads(q, kh, group)
        keys = k[:, kh * HD : (kh + 1) * HD]
        scores = lax.dot_general(
            keys, queries, (((1,), (1,)), ((), ())), preferred_element_type=jnp.float32
        ) / jnp.sqrt(jnp.float32(HD))
        masked = jnp.where(allowed, scores, -jnp.inf)
        top = jnp.max(masked, axis=0, keepdims=True)
        weights = jnp.where(allowed, jnp.exp(masked - top), 0.0)
        share = weights / jnp.sum(weights, axis=0, keepdims=True)
        share = jnp.where(live, share, 0.0)
        shares.append(share)
        share = share.astype(jnp.bfloat16)
        grads = stack_heads(og, kh, group)
        part = jnp.dot(share, grads, preferred_element_type=jnp.float32)
        part = (part * scale).astype(jnp.bfloat16)
        dv[:, kh * HD : (kh + 1) * HD] = part
        held[colours[s], :, kh * HD : (kh + 1) * HD] = part
    probs[0] = jnp.concatenate(shares, axis=0).T.astype(jnp.bfloat16)

    @pl.when(s == slots - 1)
    def _():
        turned[...] = held[...].reshape(slots * seq, kv * HD).T


def probs_and_dvalues(length, colours, factor, queries, keys, out_grad, slots):
    tokens, width = queries.shape
    seq = tokens // slots
    kv = keys.shape[1] // HD
    group = width // HD // kv
    return pl.pallas_call(
        functools.partial(probs_body, kv, group, slots),
        grid_spec=pltpu.PrefetchScalarGridSpec(
            num_scalar_prefetch=2,
            grid=(slots,),
            in_specs=[
                pl.BlockSpec((slots, 128), lambda s, n, c: (0, 0)),
                pl.BlockSpec((seq, width), lambda s, n, c: (s, 0)),
                pl.BlockSpec((seq, keys.shape[1]), lambda s, n, c: (s, 0)),
                pl.BlockSpec((seq, width), lambda s, n, c: (s, 0)),
            ],
            out_specs=[
                pl.BlockSpec((seq, keys.shape[1]), lambda s, n, c: (s, 0)),
                pl.BlockSpec((keys.shape[1], tokens), lambda s, n, c: (0, 0)),
                pl.BlockSpec((1, group * seq, kv * seq), lambda s, n, c: (s, 0, 0)),
            ],
            scratch_shapes=[pltpu.VMEM((slots, seq, keys.shape[1]), jnp.bfloat16)],
        ),
        out_shape=[
            jax.ShapeDtypeStruct((tokens, keys.shape[1]), jnp.bfloat16),
            jax.ShapeDtypeStruct((keys.shape[1], tokens), jnp.bfloat16),
            jax.ShapeDtypeStruct((slots, group * seq, kv * seq), jnp.bfloat16),
        ],
        compiler_params=params(),
        cost_estimate=pl.CostEstimate(flops=1, bytes_accessed=1, transcendentals=0),
        name="probs_dvalues",
    )(length, colours, factor, queries, keys, out_grad)


def values_body(steps, where, rows, near, far, out, acc):
    step = pl.program_id(0)
    dp, _, low, seq, part = rows.shape
    total = jnp.zeros(acc.shape, jnp.float32)
    for c in range(low):
        for w, h in ((near, where[2]), (far, 1 - where[2])):
            x = rows[:, h, c].reshape(dp * seq, part)
            total += jnp.dot(x, w[c], preferred_element_type=jnp.float32)

    @pl.when(step == 0)
    def _():
        acc[...] = total

    @pl.when(step > 0)
    def _():
        acc[...] += total

    @pl.when(step == steps - 1)
    def _():
        out[...] = acc[...].astype(out.dtype).reshape(out.shape)


def values_of(where, rows, near, far):
    dp, high, low, seq, part = rows.shape
    cols = near.shape[2]
    each = 2
    steps = low // each
    return pl.pallas_call(
        functools.partial(values_body, steps),
        grid_spec=pltpu.PrefetchScalarGridSpec(
            num_scalar_prefetch=1,
            grid=(steps,),
            in_specs=[pl.BlockSpec((dp, high, each, seq, part), lambda i, n: (0, 0, i, 0, 0))]
            + [pl.BlockSpec((each, part, cols), lambda i, n: (i, 0, 0))] * 2,
            out_specs=pl.BlockSpec((dp, seq, cols), lambda i, n: (0, 0, 0)),
            scratch_shapes=[pltpu.VMEM((dp * seq, cols), jnp.float32)],
        ),
        out_shape=jax.ShapeDtypeStruct((dp, seq, cols), jnp.bfloat16),
        compiler_params=params(),
        cost_estimate=pl.CostEstimate(flops=1, bytes_accessed=1, transcendentals=0),
        name="values",
    )(where, rows, near, far)


def grad_rows_body(where, dv, near, far, out):
    each, part, _ = near.shape
    half = pl.program_id(0)

    def write(w):
        for c in range(each):
            out[:, c * part : (c + 1) * part] = lax.dot_general(
                dv[...], w[c], (((1,), (1,)), ((), ())), preferred_element_type=jnp.float32
            ).astype(out.dtype)

    @pl.when(half == 0)
    def _():
        write(near)

    @pl.when(half == 1)
    def _():
        write(far)


def grad_rows_of(where, dv, near, far):
    tokens, cols = dv.shape
    low, part, _ = near.shape
    each = 4
    steps = low // each
    return pl.pallas_call(
        grad_rows_body,
        grid_spec=pltpu.PrefetchScalarGridSpec(
            num_scalar_prefetch=1,
            grid=(2, steps),
            in_specs=[
                pl.BlockSpec((tokens, cols), lambda h, i, n: (0, 0)),
                pl.BlockSpec((each, part, cols), lambda h, i, n: (i * (1 - h) + (steps - 1) * h, 0, 0)),
                pl.BlockSpec((each, part, cols), lambda h, i, n: (i * h, 0, 0)),
            ],
            out_specs=pl.BlockSpec(
                (tokens, each * part), lambda h, i, n: (0, lax.rem(n[2] + h, 2) * steps + i)
            ),
        ),
        out_shape=jax.ShapeDtypeStruct((tokens, 2 * low * part), jnp.bfloat16),
        compiler_params=params(),
        cost_estimate=pl.CostEstimate(flops=1, bytes_accessed=1, transcendentals=0),
        name="grad_rows",
    )(where, dv, near, far)


def attend_body(kv, group, dp, each, colours, where, probs, *rest):
    values, out, held = rest[:dp], rest[dp], rest[dp + 1]
    step = pl.program_id(0)
    seq, cols = values[0].shape

    @pl.when(step == 0)
    def _():
        for k in range(dp):
            held[k] = values[k][...]

    for e in range(each):
        away = lax.rem(where[1] - colours[step * each + e] + dp, dp)
        mine = held[away]
        zero = jnp.zeros((seq, HD), mine.dtype)
        blocks = []
        for kh in range(kv):
            row = [zero] * kv
            row[kh] = mine[:, kh * HD : (kh + 1) * HD]
            blocks.append(jnp.concatenate(row, axis=1))
        heads = jnp.dot(
            probs[e], jnp.concatenate(blocks, axis=0), preferred_element_type=jnp.float32
        ).astype(out.dtype)
        for kh in range(kv):
            for g in range(group):
                h = kh * group + g
                out[e * seq : (e + 1) * seq, h * HD : (h + 1) * HD] = heads[
                    g * seq : (g + 1) * seq, kh * HD : (kh + 1) * HD
                ]


def attend(colours, where, probs, values):
    slots, span, keys = probs.shape
    seq, cols = values[0].shape
    kv = cols // HD
    group = span // seq
    width = kv * group * HD
    dp = len(values)
    each = 2
    return pl.pallas_call(
        functools.partial(attend_body, kv, group, dp, each),
        grid_spec=pltpu.PrefetchScalarGridSpec(
            num_scalar_prefetch=2,
            grid=(slots // each,),
            in_specs=[pl.BlockSpec((each, span, keys), lambda s, c, w: (s, 0, 0))]
            + [pl.BlockSpec((seq, cols), lambda s, c, w: (0, 0))] * dp,
            out_specs=pl.BlockSpec((each * seq, width), lambda s, c, w: (s, 0)),
            scratch_shapes=[pltpu.VMEM((dp, seq, cols), jnp.bfloat16)],
        ),
        out_shape=jax.ShapeDtypeStruct((slots * seq, width), jnp.bfloat16),
        compiler_params=params(),
        cost_estimate=pl.CostEstimate(flops=1, bytes_accessed=1, transcendentals=0),
        name="attend",
    )(colours, where, probs, *values)


def product_body(steps, scale, where, near_rows, far_rows, near, far, out, acc):
    step = pl.program_id(0)
    colours, _, each, seq, width = near_rows.shape
    part = jnp.zeros(acc.shape, jnp.float32)
    for rows, dv in ((near_rows, near), (far_rows, far)):
        for b in range(each):
            x = rows[:, 0, b].reshape(colours * seq, width)
            part += jnp.dot(dv[b], x, preferred_element_type=jnp.float32)

    @pl.when(step == 0)
    def _():
        acc[...] = part

    @pl.when(step > 0)
    def _():
        acc[...] += part

    @pl.when(step == steps - 1)
    def _():
        out[...] = (acc[...] * scale).T.astype(out.dtype)


def product(where, rows, near, far, scale):
    colours, _, low, seq, width = rows.shape
    cols = near.shape[1]
    each = 2
    steps = low // each
    return pl.pallas_call(
        functools.partial(product_body, steps, scale),
        grid_spec=pltpu.PrefetchScalarGridSpec(
            num_scalar_prefetch=1,
            grid=(steps,),
            in_specs=[
                pl.BlockSpec((colours, 1, each, seq, width), lambda i, n: (0, n[2], i, 0, 0)),
                pl.BlockSpec((colours, 1, each, seq, width), lambda i, n: (0, 1 - n[2], i, 0, 0)),
                pl.BlockSpec((each, cols, colours * seq), lambda i, n: (i, 0, 0)),
                pl.BlockSpec((each, cols, colours * seq), lambda i, n: (i, 0, 0)),
            ],
            out_specs=pl.BlockSpec((width, cols), lambda i, n: (0, 0)),
            scratch_shapes=[pltpu.VMEM((cols, width), jnp.float32)],
        ),
        out_shape=jax.ShapeDtypeStruct((width, cols), jnp.bfloat16),
        compiler_params=params(),
        cost_estimate=pl.CostEstimate(
            flops=2 * rows.size * cols,
            bytes_accessed=2 * (2 * rows.size + width * cols),
            transcendentals=0,
        ),
        name="weight_product",
    )(where, rows, rows, near, far)


def shards(
    rollout_rows, rewards, group_ids, lengths, packing, queries, keys, out_grad, value_weight
):
    slots, seq, width = rollout_rows.shape
    dp = lax.axis_size("dp")
    fsdp = lax.axis_size("fsdp")
    part = width // fsdp
    home = lax.axis_index("dp")
    place = lax.axis_index("fsdp")
    where = jnp.stack([home * fsdp + place, home, lax.div(place, fsdp // 2)]).astype(jnp.int32)
    info, order = prepare(where, packing, lengths, rewards, group_ids, dp, fsdp)
    info = lax.all_to_all(info, ("dp", "fsdp"), split_axis=0, concat_axis=0, tiled=True)
    rows = pack(order, rollout_rows, fsdp)
    low = fsdp // 2
    halves = [list(range(low)), list(range(low, fsdp))]
    swap = [(i, (i + low) % fsdp) for i in range(fsdp)]
    far_weight = lax.ppermute(value_weight, "fsdp", swap)
    rows, info, far_weight = lax.optimization_barrier((rows, info, far_weight))
    rows = lax.all_to_all(
        rows.reshape(dp, fsdp * seq, part), "dp", split_axis=0, concat_axis=0, tiled=True
    )
    near = lax.all_gather(value_weight, "fsdp", axis_index_groups=halves)
    far = lax.all_gather(far_weight, "fsdp", axis_index_groups=halves)
    length, colours, factor = plan(where, info.T, slots, dp, fsdp, seq)
    dvalues, coloured, probs = probs_and_dvalues(
        length, colours, factor, queries, keys, out_grad, slots
    )
    rows, dvalues, probs = lax.optimization_barrier((rows, dvalues, probs))
    far_dv = lax.ppermute(coloured, "fsdp", swap)
    rows = turn(order, rows)
    rows, far_dv = lax.optimization_barrier((rows, far_dv))
    coloured, near, far = lax.optimization_barrier((coloured, near, far))
    near_dv = lax.all_gather(coloured, "fsdp", axis_index_groups=halves)
    far_dv = lax.all_gather(far_dv, "fsdp", axis_index_groups=halves)
    values = values_of(where, rows.reshape(dp, 2, low, seq, part), near, far)
    grad_rows = grad_rows_of(where, dvalues, near, far)
    held = [
        lax.dynamic_index_in_dim(values, lax.rem(home + k, dp), 0, keepdims=False)
        for k in range(dp)
    ]
    held = [held[0]] + [
        lax.ppermute(held[k], "dp", [(i, (i + k) % dp) for i in range(dp)])
        for k in range(1, dp)
    ]
    rows = lax.all_to_all(
        rows.reshape(dp * fsdp, seq, part),
        ("dp", "fsdp"),
        split_axis=0,
        concat_axis=0,
        tiled=True,
    )
    rows, grad_rows = lax.optimization_barrier((rows, grad_rows))
    grad_weight = product(
        where, rows.reshape(dp, 2, low, seq, part), near_dv, far_dv, 1.0 / fsdp
    )[None]
    attn_out = attend(colours, where, probs, held)
    return (attn_out, grad_rows, grad_weight)


def solution(mesh):
    in_specs = (
        P(("dp", "fsdp"), None, None),
        P(("dp", "fsdp")),
        P(("dp", "fsdp")),
        P(("dp", "fsdp")),
        P(("dp", "fsdp")),
        P(("dp", "fsdp"), None),
        P(("dp", "fsdp"), None),
        P(("dp", "fsdp"), None),
        P("fsdp", None),
    )
    out_specs = (P(("dp", "fsdp"), None), P(("dp", "fsdp"), None), P("dp", "fsdp", None))
    return jax.shard_map(shards, mesh=mesh, in_specs=in_specs, out_specs=out_specs, check_vma=False)
```

```python
import functools

import jax
import jax.numpy as jnp
from jax import lax
from jax.experimental import pallas as pl
from jax.experimental.pallas import tpu as pltpu
from jax.sharding import PartitionSpec as P

HD = 128
VMEM = 56 * 1024 * 1024


def params(**kw):
    return pltpu.CompilerParams(vmem_limit_bytes=VMEM, **kw)


def prepare_body(slots, dp, fsdp, packing, lengths, rewards, groups, info, order):
    lane = lax.broadcasted_iota(jnp.int32, info.shape, 1)
    told = jnp.zeros(info.shape, jnp.float32)
    for r in range(slots):
        told = jnp.where(lane == r, packing[r].astype(jnp.float32), told)
        told = jnp.where(lane == slots + r, lengths[r].astype(jnp.float32), told)
        told = jnp.where(lane == 2 * slots + r, rewards[r], told)
        told = jnp.where(lane == 3 * slots + r, groups[r].astype(jnp.float32), told)
    info[...] = told
    home = lax.axis_index("dp")
    offsets = [lax.rem(lax.div(packing[r], slots * fsdp) - home + dp, dp) for r in range(slots)]
    mine = jnp.int32(0)
    for r in range(slots):
        colour = jnp.int32(0)
        for k in range(slots):
            if k != r:
                first = offsets[k] <= offsets[r] if k < r else offsets[k] < offsets[r]
                colour = colour + jnp.where(first, 1, 0)
        order[r] = colour
        mine = mine + jnp.where(colour == home, offsets[r], 0)
    order[slots] = mine


def prepare(packing, lengths, rewards, groups, dp, fsdp):
    slots = packing.shape[0]
    smem = pl.BlockSpec(memory_space=pltpu.SMEM)
    return pl.pallas_call(
        functools.partial(prepare_body, slots, dp, fsdp),
        in_specs=[smem] * 4,
        out_specs=[pl.BlockSpec(memory_space=pltpu.VMEM), smem],
        out_shape=[
            jax.ShapeDtypeStruct((dp * fsdp, 4 * slots), jnp.float32),
            jax.ShapeDtypeStruct((slots + 1,), jnp.int32),
        ],
        name="prepare",
    )(packing, lengths, rewards, groups)


def pack_body(fsdp, order, rows, out, held, cut, arrive, leave):
    slots, _, width = rows.shape
    part = width // fsdp
    ins = [pltpu.make_async_copy(rows.at[r], held.at[r], arrive.at[r]) for r in range(slots)]
    outs = [pltpu.make_async_copy(cut.at[r], out.at[order[r]], leave.at[r]) for r in range(slots)]
    half = fsdp // 2
    for copy in ins:
        copy.start()
    for r in range(slots):
        ins[r].wait()
        for f in range(fsdp):
            cut[r, f % half * 2 + f // half] = held[r, :, f * part : (f + 1) * part]
        outs[r].start()
    for copy in outs:
        copy.wait()


def pack(order, rows, fsdp):
    slots, seq, width = rows.shape
    part = width // fsdp
    return pl.pallas_call(
        functools.partial(pack_body, fsdp),
        in_specs=[pl.BlockSpec(memory_space=pltpu.SMEM), pl.BlockSpec(memory_space=pl.ANY)],
        out_specs=pl.BlockSpec(memory_space=pl.ANY),
        out_shape=jax.ShapeDtypeStruct((slots, fsdp, seq, part), rows.dtype),
        scratch_shapes=[
            pltpu.VMEM((slots, seq, width), rows.dtype),
            pltpu.VMEM((slots, fsdp, seq, part), rows.dtype),
            pltpu.SemaphoreType.DMA((slots,)),
            pltpu.SemaphoreType.DMA((slots,)),
        ],
        compiler_params=params(),
        cost_estimate=pl.CostEstimate(
            flops=0, bytes_accessed=2 * rows.size * 2, transcendentals=0
        ),
        name="pack_rows",
    )(order, rows)


def turn_body(dp, slots, order, rows, out, held, arrive, leave):
    ins = [pltpu.make_async_copy(rows.at[p], held.at[p], arrive.at[p]) for p in range(dp)]
    outs = []
    for p in range(dp):
        dest = lax.rem(order[slots] + p, dp)
        outs.append(pltpu.make_async_copy(held.at[p], out.at[dest], leave.at[p]))
    for copy in ins:
        copy.start()
    for p in range(dp):
        ins[p].wait()
        outs[p].start()
    for copy in outs:
        copy.wait()


def turn(order, rows):
    dp = rows.shape[0]
    return pl.pallas_call(
        functools.partial(turn_body, dp, order.shape[0] - 1),
        in_specs=[pl.BlockSpec(memory_space=pltpu.SMEM), pl.BlockSpec(memory_space=pl.ANY)],
        out_specs=pl.BlockSpec(memory_space=pl.ANY),
        out_shape=jax.ShapeDtypeStruct(rows.shape, rows.dtype),
        scratch_shapes=[
            pltpu.VMEM(rows.shape, rows.dtype),
            pltpu.SemaphoreType.DMA((dp,)),
            pltpu.SemaphoreType.DMA((dp,)),
        ],
        compiler_params=params(),
        cost_estimate=pl.CostEstimate(
            flops=0, bytes_accessed=2 * rows.size * 2, transcendentals=0
        ),
        name="turn_rows",
    )(order, rows)


def plan_body(slots, dp, fsdp, seq, me, info, length, colours, factor):
    told = info[...].T
    packing = told[0:slots, :]
    lengths = told[slots : 2 * slots, :]
    rewards = told[2 * slots : 3 * slots, :]
    groups = told[3 * slots : 4 * slots, :]
    lane = lax.broadcasted_iota(jnp.int32, packing.shape, 1)
    row = lax.broadcasted_iota(jnp.int32, packing.shape, 0)
    target = lax.div(packing.astype(jnp.int32), slots * fsdp)

    offset = lax.rem(target - lax.div(lane, fsdp) + dp, dp)
    colour = jnp.zeros(packing.shape, jnp.int32)
    for k in range(1, slots):
        other = pltpu.roll(offset, k, 0)
        first = (other < offset) | ((other == offset) & (row >= k))
        colour = colour + jnp.where(first, 1, 0)
    colour = colour.astype(jnp.float32)

    def total(x):
        return jnp.sum(jnp.sum(x, axis=0, keepdims=True), axis=1, keepdims=True)

    for s in range(slots):
        hit = jnp.where(packing == (me[0] * slots + s).astype(jnp.float32), 1.0, 0.0)
        size = total(hit * lengths)
        reward = total(hit * rewards)
        same = jnp.where(groups == total(hit * groups), 1.0, 0.0)
        mean = total(same * rewards) / jnp.maximum(total(same), 1.0)
        advantage = (reward - mean).astype(jnp.bfloat16).astype(jnp.float32)
        factor[s : s + 1, :] = jnp.broadcast_to(-advantage * seq / size, (1, 128))
        colours[s] = total(hit * colour)[0, 0].astype(jnp.int32)
        length[s] = size[0, 0].astype(jnp.int32)


def plan(me, info, slots, dp, fsdp, seq):
    smem = pl.BlockSpec(memory_space=pltpu.SMEM)
    vmem = pl.BlockSpec(memory_space=pltpu.VMEM)
    return pl.pallas_call(
        functools.partial(plan_body, slots, dp, fsdp, seq),
        in_specs=[smem, vmem],
        out_specs=[smem, smem, vmem],
        out_shape=[
            jax.ShapeDtypeStruct((slots,), jnp.int32),
            jax.ShapeDtypeStruct((slots,), jnp.int32),
            jax.ShapeDtypeStruct((slots, 128), jnp.float32),
        ],
        cost_estimate=pl.CostEstimate(flops=1, bytes_accessed=1, transcendentals=0),
        name="plan_slots",
    )(me, info)


def stack_heads(ref, kh, group):
    cols = [ref[:, (kh * group + g) * HD : (kh * group + g + 1) * HD] for g in range(group)]
    return jnp.concatenate(cols, axis=0)


def probs_body(kv, group, slots, length, colours, factor, q, k, og, dv, turned, probs, held):
    s = pl.program_id(0)
    seq = q.shape[0]
    size = length[s]
    scale = factor[pl.ds(s, 1), :]
    key_pos = lax.broadcasted_iota(jnp.int32, (seq, group * seq), 0)
    query_pos = lax.rem(lax.broadcasted_iota(jnp.int32, (seq, group * seq), 1), seq)
    allowed = (key_pos <= query_pos) & (key_pos < size)
    live = query_pos < size
    shares = []
    for kh in range(kv):
        queries = stack_heads(q, kh, group)
        keys = k[:, kh * HD : (kh + 1) * HD]
        scores = lax.dot_general(
            keys, queries, (((1,), (1,)), ((), ())), preferred_element_type=jnp.float32
        ) / jnp.sqrt(jnp.float32(HD))
        masked = jnp.where(allowed, scores, -jnp.inf)
        top = jnp.max(masked, axis=0, keepdims=True)
        weights = jnp.where(allowed, jnp.exp(masked - top), 0.0)
        share = weights / jnp.sum(weights, axis=0, keepdims=True)
        share = jnp.where(live, share, 0.0)
        shares.append(share)
        share = share.astype(jnp.bfloat16)
        grads = stack_heads(og, kh, group)
        part = jnp.dot(share, grads, preferred_element_type=jnp.float32)
        part = (part * scale).astype(jnp.bfloat16)
        dv[:, kh * HD : (kh + 1) * HD] = part
        held[colours[s], :, kh * HD : (kh + 1) * HD] = part
    probs[0] = jnp.concatenate(shares, axis=0).T.astype(jnp.bfloat16)

    @pl.when(s == slots - 1)
    def _():
        turned[...] = held[...].reshape(slots * seq, kv * HD).T


def probs_and_dvalues(length, colours, factor, queries, keys, out_grad, slots):
    tokens, width = queries.shape
    seq = tokens // slots
    kv = keys.shape[1] // HD
    group = width // HD // kv
    return pl.pallas_call(
        functools.partial(probs_body, kv, group, slots),
        grid_spec=pltpu.PrefetchScalarGridSpec(
            num_scalar_prefetch=2,
            grid=(slots,),
            in_specs=[
                pl.BlockSpec((slots, 128), lambda s, n, c: (0, 0)),
                pl.BlockSpec((seq, width), lambda s, n, c: (s, 0)),
                pl.BlockSpec((seq, keys.shape[1]), lambda s, n, c: (s, 0)),
                pl.BlockSpec((seq, width), lambda s, n, c: (s, 0)),
            ],
            out_specs=[
                pl.BlockSpec((seq, keys.shape[1]), lambda s, n, c: (s, 0)),
                pl.BlockSpec((keys.shape[1], tokens), lambda s, n, c: (0, 0)),
                pl.BlockSpec((1, group * seq, kv * seq), lambda s, n, c: (s, 0, 0)),
            ],
            scratch_shapes=[pltpu.VMEM((slots, seq, keys.shape[1]), jnp.bfloat16)],
        ),
        out_shape=[
            jax.ShapeDtypeStruct((tokens, keys.shape[1]), jnp.bfloat16),
            jax.ShapeDtypeStruct((keys.shape[1], tokens), jnp.bfloat16),
            jax.ShapeDtypeStruct((slots, group * seq, kv * seq), jnp.bfloat16),
        ],
        compiler_params=params(),
        cost_estimate=pl.CostEstimate(flops=1, bytes_accessed=1, transcendentals=0),
        name="probs_dvalues",
    )(length, colours, factor, queries, keys, out_grad)


def values_body(steps, where, rows, *rest):
    weights, out, acc = rest[:4], rest[4], rest[5]
    step = pl.program_id(0)
    dp, _, _, _, seq, part = rows.shape
    lhs, rhs = [], []
    for n, w in enumerate(weights):
        x = rows[:, 0, lax.rem(where[4] + n // 2, 2), lax.rem(where[2] + n % 2, 2)]
        lhs.append(x.reshape(dp * seq, part))
        rhs.append(w[0])
    total = jnp.dot(
        jnp.concatenate(lhs, axis=1),
        jnp.concatenate(rhs, axis=0),
        preferred_element_type=jnp.float32,
    )

    @pl.when(step == 0)
    def _():
        acc[...] = total

    @pl.when(step > 0)
    def _():
        acc[...] += total

    @pl.when(step == steps - 1)
    def _():
        out[...] = acc[...].astype(out.dtype).reshape(out.shape)


def values_of(where, rows, weights):
    dp, around, cores, high, seq, part = rows.shape
    cols = weights[0].shape[2]
    return pl.pallas_call(
        functools.partial(values_body, around),
        grid_spec=pltpu.PrefetchScalarGridSpec(
            num_scalar_prefetch=1,
            grid=(around,),
            in_specs=[
                pl.BlockSpec(
                    (dp, 1, cores, high, seq, part),
                    lambda i, n: (0, lax.rem(n[3] - i + around, around), 0, 0, 0, 0),
                )
            ]
            + [pl.BlockSpec((1, part, cols), lambda i, n: (i, 0, 0))] * 4,
            out_specs=pl.BlockSpec((dp, seq, cols), lambda i, n: (0, 0, 0)),
            scratch_shapes=[pltpu.VMEM((dp * seq, cols), jnp.float32)],
        ),
        out_shape=jax.ShapeDtypeStruct((dp, seq, cols), jnp.bfloat16),
        compiler_params=params(),
        cost_estimate=pl.CostEstimate(flops=1, bytes_accessed=1, transcendentals=0),
        name="values",
    )(where, rows, *weights)


def grad_rows_body(where, dv, *rest):
    weights, outs = rest[:4], rest[4]
    part = weights[0].shape[1]
    half = pl.program_id(0)

    def write(first, second):
        for c, w in enumerate((first, second)):
            outs[:, c * part : (c + 1) * part] = lax.dot_general(
                dv[...], w[0], (((1,), (1,)), ((), ())), preferred_element_type=jnp.float32
            ).astype(outs.dtype)

    for h in range(2):
        for c in range(2):

            @pl.when((half == h) & (where[4] == c))
            def _(h=h, c=c):
                write(weights[2 * c + h], weights[2 * (1 - c) + h])


def grad_rows_of(where, dv, weights):
    tokens, cols = dv.shape
    around, part, _ = weights[0].shape
    last = around - 1
    near = pl.BlockSpec((1, part, cols), lambda h, i, n: (i * (1 - h) + last * h, 0, 0))
    far = pl.BlockSpec((1, part, cols), lambda h, i, n: (i * h, 0, 0))
    return pl.pallas_call(
        grad_rows_body,
        grid_spec=pltpu.PrefetchScalarGridSpec(
            num_scalar_prefetch=1,
            grid=(2, around),
            in_specs=[pl.BlockSpec((tokens, cols), lambda h, i, n: (0, 0)), near, far, near, far],
            out_specs=pl.BlockSpec(
                (tokens, 2 * part),
                lambda h, i, n: (
                    0,
                    lax.rem(n[2] + h, 2) * around + lax.rem(n[3] - i + around, around),
                ),
            ),
        ),
        out_shape=jax.ShapeDtypeStruct((tokens, 4 * around * part), jnp.bfloat16),
        compiler_params=params(),
        cost_estimate=pl.CostEstimate(flops=1, bytes_accessed=1, transcendentals=0),
        name="grad_rows",
    )(where, dv, *weights)


def attend_body(kv, group, levels, each, colours, where, probs, *rest):
    values, out, held = rest[:levels], rest[levels], rest[levels + 1]
    step = pl.program_id(0)
    _, seq, cols = values[0].shape

    @pl.when(step == 0)
    def _():
        for k in range(levels):
            held[2 * k : 2 * k + 2] = values[k][...]

    for e in range(each):
        colour = colours[step * each + e]
        away = lax.rem(where[1] - colour + 2 * levels, levels)
        other = lax.rem(lax.div(where[1], levels) + lax.div(colour, levels), 2)
        mine = held[2 * away + other]
        zero = jnp.zeros((seq, HD), mine.dtype)
        blocks = []
        for kh in range(kv):
            row = [zero] * kv
            row[kh] = mine[:, kh * HD : (kh + 1) * HD]
            blocks.append(jnp.concatenate(row, axis=1))
        heads = jnp.dot(
            probs[e], jnp.concatenate(blocks, axis=0), preferred_element_type=jnp.float32
        ).astype(out.dtype)
        for kh in range(kv):
            for g in range(group):
                h = kh * group + g
                out[e * seq : (e + 1) * seq, h * HD : (h + 1) * HD] = heads[
                    g * seq : (g + 1) * seq, kh * HD : (kh + 1) * HD
                ]


def attend(colours, where, probs, values):
    slots, span, keys = probs.shape
    _, seq, cols = values[0].shape
    kv = cols // HD
    group = span // seq
    width = kv * group * HD
    levels = len(values)
    each = 2
    return pl.pallas_call(
        functools.partial(attend_body, kv, group, levels, each),
        grid_spec=pltpu.PrefetchScalarGridSpec(
            num_scalar_prefetch=2,
            grid=(slots // each,),
            in_specs=[pl.BlockSpec((each, span, keys), lambda s, c, w: (s, 0, 0))]
            + [pl.BlockSpec((2, seq, cols), lambda s, c, w: (0, 0, 0))] * levels,
            out_specs=pl.BlockSpec((each * seq, width), lambda s, c, w: (s, 0)),
            scratch_shapes=[pltpu.VMEM((2 * levels, seq, cols), jnp.bfloat16)],
        ),
        out_shape=jax.ShapeDtypeStruct((slots * seq, width), jnp.bfloat16),
        compiler_params=params(),
        cost_estimate=pl.CostEstimate(flops=1, bytes_accessed=1, transcendentals=0),
        name="attend",
    )(colours, where, probs, *values)


def product_body(scale, where, rows, near, far, out):
    colours, around, _, _, seq, width = rows.shape
    lhs, rhs = [], []
    for k in range(around):
        for other, dv in enumerate((near, far)):
            x = rows[:, lax.rem(where[3] - k + around, around), lax.rem(where[4] + other, 2), 0]
            rhs.append(x.reshape(colours * seq, width))
            lhs.append(dv[k])
    part = jnp.dot(
        jnp.concatenate(lhs, axis=1),
        jnp.concatenate(rhs, axis=0),
        preferred_element_type=jnp.float32,
    )
    out[...] = (part * scale).T.astype(out.dtype)


def product(where, rows, near, far, scale, apart, dtype):
    colours, around, cores, high, seq, width = rows.shape
    _, cols, tokens = near.shape
    return pl.pallas_call(
        functools.partial(product_body, scale),
        grid_spec=pltpu.PrefetchScalarGridSpec(
            num_scalar_prefetch=1,
            grid=(1,),
            in_specs=[
                pl.BlockSpec(
                    (colours, around, cores, 1, seq, width),
                    lambda i, n: (0, 0, 0, lax.rem(n[2] + apart, high), 0, 0),
                )
            ]
            + [pl.BlockSpec((around, cols, tokens), lambda i, n: (0, 0, 0))] * 2,
            out_specs=pl.BlockSpec((width, cols), lambda i, n: (0, 0)),
        ),
        out_shape=jax.ShapeDtypeStruct((width, cols), dtype),
        compiler_params=params(),
        cost_estimate=pl.CostEstimate(flops=1, bytes_accessed=1, transcendentals=0),
        name="weight_product",
    )(where, rows, near, far)


def swap_rows(x, fsdp):
    return lax.ppermute(x, "fsdp", [(i, (i + fsdp // 2) % fsdp) for i in range(fsdp)])


def step_along(x, fsdp, step):
    half = fsdp // 2
    to = [(i, i // half * half + (i + 2 * step) % half) for i in range(fsdp)]
    return lax.ppermute(x, "fsdp", to)


def neighbours(x, fsdp):
    return step_along(x, fsdp, 1), step_along(x, fsdp, -1)


def opposite(back, front, fsdp):
    middle = back.shape[0] // 2
    return jnp.concatenate(
        [step_along(back[:middle], fsdp, 1), step_along(front[middle:], fsdp, -1)], axis=0
    )


def swap_cores(x, fsdp):
    return lax.ppermute(x, "fsdp", [(i, i ^ 1) for i in range(fsdp)])


def shards(
    rollout_rows, rewards, group_ids, lengths, packing, queries, keys, out_grad, value_weight
):
    slots, seq, width = rollout_rows.shape
    dp = lax.axis_size("dp")
    fsdp = lax.axis_size("fsdp")
    part = width // fsdp
    home = lax.axis_index("dp")
    place = lax.axis_index("fsdp")
    around = fsdp // 4
    where = jnp.stack(
        [home * fsdp + place, home, place // (2 * around), place // 2 % around, place % 2]
    ).astype(jnp.int32)
    info, order = prepare(packing, lengths, rewards, group_ids, dp, fsdp)
    info = lax.all_to_all(info, ("dp", "fsdp"), split_axis=0, concat_axis=0, tiled=True)
    rows = pack(order, rollout_rows, fsdp)
    across = swap_rows(value_weight, fsdp)
    back, front = neighbours(value_weight, fsdp)
    rows, info, across, back, front = lax.optimization_barrier(
        (rows, info, across, back, front)
    )
    rows = lax.all_to_all(
        rows.reshape(dp, fsdp * seq, part), "dp", split_axis=0, concat_axis=0, tiled=True
    )
    own = [value_weight, back, opposite(back, front, fsdp), front]
    across_back, across_front = neighbours(across, fsdp)
    length, colours, factor = plan(where, info, slots, dp, fsdp, seq)
    dvalues, turned, probs = probs_and_dvalues(
        length, colours, factor, queries, keys, out_grad, slots
    )
    dv_back, dv_front = neighbours(turned, fsdp)
    across_way = opposite(across_back, across_front, fsdp)
    across = [across, across_back, across_way, across_front]
    own, dvalues = lax.optimization_barrier((own, dvalues))
    own = jnp.stack(own)
    own_far = swap_cores(own, fsdp)
    across = jnp.stack(across)
    across_far = swap_cores(across, fsdp)
    weights = (own, across, own_far, across_far)
    near_dv = jnp.stack([turned, dv_back, opposite(dv_back, dv_front, fsdp), dv_front])
    far_dv = swap_cores(near_dv, fsdp)
    rows, dvalues, probs, weights, near_dv, far_dv = lax.optimization_barrier(
        (rows, dvalues, probs, weights, near_dv, far_dv)
    )
    rows = turn(order, rows)
    half = fsdp // 2
    groups = [
        [d * fsdp + h * half + i for d in range(dp) for i in range(half)] for h in range(2)
    ]
    sent = rows
    rows = lax.all_to_all(
        rows.reshape(dp * half, 2 * seq, part),
        ("dp", "fsdp"),
        split_axis=0,
        concat_axis=0,
        axis_index_groups=groups,
        tiled=True,
    ).reshape(dp, around, 2, 2, seq, part)
    grad_rows = grad_rows_of(where, dvalues, weights)
    sent, grad_rows = lax.optimization_barrier((sent, grad_rows))
    values = values_of(where, sent.reshape(dp, around, 2, 2, seq, part), weights)
    side, level = home // 4, home % 4
    keep = lax.dynamic_slice_in_dim(values, side * 4, 4, 0)
    give = lax.dynamic_slice_in_dim(values, (1 - side) * 4, 4, 0)
    got = lax.ppermute(give, "dp", [(i, (i + 4) % dp) for i in range(dp)])
    rows, got = lax.optimization_barrier((rows, got))
    both = [
        jnp.stack([lax.dynamic_index_in_dim(v, (level + k) % 4, 0, False) for v in (keep, got)])
        for k in range(4)
    ]
    held = [both[0]] + [
        lax.ppermute(both[k], "dp", [(i, i // 4 * 4 + (i + k) % 4) for i in range(dp)])
        for k in range(1, 4)
    ]
    given = product(where, rows, near_dv, far_dv, 1.0 / fsdp, 1, jnp.bfloat16)
    rows, given = lax.optimization_barrier((rows, given))
    given = swap_rows(given, fsdp)
    own = product(where, rows, near_dv, far_dv, 1.0 / fsdp, 0, jnp.float32)
    attn_out = attend(colours, where, probs, held)
    given, own, attn_out = lax.optimization_barrier((given, own, attn_out))
    grad_weight = (own + given.astype(jnp.float32)).astype(jnp.bfloat16)[None]
    return (attn_out, grad_rows, grad_weight)


def solution(mesh):
    in_specs = (
        P(("dp", "fsdp"), None, None),
        P(("dp", "fsdp")),
        P(("dp", "fsdp")),
        P(("dp", "fsdp")),
        P(("dp", "fsdp")),
        P(("dp", "fsdp"), None),
        P(("dp", "fsdp"), None),
        P(("dp", "fsdp"), None),
        P("fsdp", None),
    )
    out_specs = (P(("dp", "fsdp"), None), P(("dp", "fsdp"), None), P("dp", "fsdp", None))
    return jax.shard_map(shards, mesh=mesh, in_specs=in_specs, out_specs=out_specs, check_vma=False)
```

```python
import functools

import jax
import jax.numpy as jnp
from jax import lax
from jax.experimental import pallas as pl
from jax.experimental.pallas import tpu as pltpu
from jax.sharding import PartitionSpec as P

HD = 128
VMEM = 56 * 1024 * 1024
SMALL = 24 * 1024 * 1024


def params(limit=VMEM):
    return pltpu.CompilerParams(vmem_limit_bytes=limit)


def prepare_body(slots, dp, fsdp, packing, lengths, rewards, groups, info, order):
    lane = lax.broadcasted_iota(jnp.int32, info.shape, 1)
    told = jnp.zeros(info.shape, jnp.float32)
    for r in range(slots):
        told = jnp.where(lane == r, packing[r].astype(jnp.float32), told)
        told = jnp.where(lane == slots + r, lengths[r].astype(jnp.float32), told)
        told = jnp.where(lane == 2 * slots + r, rewards[r], told)
        told = jnp.where(lane == 3 * slots + r, groups[r].astype(jnp.float32), told)
    info[...] = told
    home = lax.axis_index("dp")
    offsets = [lax.rem(lax.div(packing[r], slots * fsdp) - home + dp, dp) for r in range(slots)]
    mine = jnp.int32(0)
    for r in range(slots):
        colour = jnp.int32(0)
        for k in range(slots):
            if k != r:
                first = offsets[k] <= offsets[r] if k < r else offsets[k] < offsets[r]
                colour = colour + jnp.where(first, 1, 0)
        order[r] = colour
        mine = mine + jnp.where(colour == home, offsets[r], 0)
    order[slots] = mine


def prepare(packing, lengths, rewards, groups, dp, fsdp):
    slots = packing.shape[0]
    smem = pl.BlockSpec(memory_space=pltpu.SMEM)
    return pl.pallas_call(
        functools.partial(prepare_body, slots, dp, fsdp),
        in_specs=[smem] * 4,
        out_specs=[pl.BlockSpec(memory_space=pltpu.VMEM), smem],
        out_shape=[
            jax.ShapeDtypeStruct((dp * fsdp, 4 * slots), jnp.float32),
            jax.ShapeDtypeStruct((slots + 1,), jnp.int32),
        ],
        name="prepare",
    )(packing, lengths, rewards, groups)


def pack_body(fsdp, order, rows, out, held, cut, arrive, leave):
    slots, _, width = rows.shape
    part = width // fsdp
    ins = [pltpu.make_async_copy(rows.at[r], held.at[r], arrive.at[r]) for r in range(slots)]
    outs = [pltpu.make_async_copy(cut.at[r], out.at[order[r]], leave.at[r]) for r in range(slots)]
    half = fsdp // 2
    for copy in ins:
        copy.start()
    for r in range(slots):
        ins[r].wait()
        for f in range(fsdp):
            cut[r, f % half * 2 + f // half] = held[r, :, f * part : (f + 1) * part]
        outs[r].start()
    for copy in outs:
        copy.wait()


def pack(order, rows, fsdp):
    slots, seq, width = rows.shape
    part = width // fsdp
    return pl.pallas_call(
        functools.partial(pack_body, fsdp),
        in_specs=[pl.BlockSpec(memory_space=pltpu.SMEM), pl.BlockSpec(memory_space=pl.ANY)],
        out_specs=pl.BlockSpec(memory_space=pl.ANY),
        out_shape=jax.ShapeDtypeStruct((slots, fsdp, seq, part), rows.dtype),
        scratch_shapes=[
            pltpu.VMEM((slots, seq, width), rows.dtype),
            pltpu.VMEM((slots, fsdp, seq, part), rows.dtype),
            pltpu.SemaphoreType.DMA((slots,)),
            pltpu.SemaphoreType.DMA((slots,)),
        ],
        compiler_params=params(),
        cost_estimate=pl.CostEstimate(
            flops=0, bytes_accessed=2 * rows.size * 2, transcendentals=0
        ),
        name="pack_rows",
    )(order, rows)


def turn_body(dp, slots, order, rows, out, held, arrive, leave):
    ins = [pltpu.make_async_copy(rows.at[p], held.at[p], arrive.at[p]) for p in range(dp)]
    outs = []
    for p in range(dp):
        dest = lax.rem(order[slots] + p, dp)
        outs.append(pltpu.make_async_copy(held.at[p], out.at[dest], leave.at[p]))
    for copy in ins:
        copy.start()
    for p in range(dp):
        ins[p].wait()
        outs[p].start()
    for copy in outs:
        copy.wait()


def turn(order, rows):
    dp = rows.shape[0]
    return pl.pallas_call(
        functools.partial(turn_body, dp, order.shape[0] - 1),
        in_specs=[pl.BlockSpec(memory_space=pltpu.SMEM), pl.BlockSpec(memory_space=pl.ANY)],
        out_specs=pl.BlockSpec(memory_space=pl.ANY),
        out_shape=jax.ShapeDtypeStruct(rows.shape, rows.dtype),
        scratch_shapes=[
            pltpu.VMEM(rows.shape, rows.dtype),
            pltpu.SemaphoreType.DMA((dp,)),
            pltpu.SemaphoreType.DMA((dp,)),
        ],
        compiler_params=params(),
        cost_estimate=pl.CostEstimate(
            flops=0, bytes_accessed=2 * rows.size * 2, transcendentals=0
        ),
        name="turn_rows",
    )(order, rows)


def plan_body(slots, dp, fsdp, seq, me, info, length, colours, factor):
    told = info[...].T
    packing = told[0:slots, :]
    lengths = told[slots : 2 * slots, :]
    rewards = told[2 * slots : 3 * slots, :]
    groups = told[3 * slots : 4 * slots, :]
    lane = lax.broadcasted_iota(jnp.int32, packing.shape, 1)
    row = lax.broadcasted_iota(jnp.int32, packing.shape, 0)
    target = lax.div(packing.astype(jnp.int32), slots * fsdp)

    offset = lax.rem(target - lax.div(lane, fsdp) + dp, dp)
    colour = jnp.zeros(packing.shape, jnp.int32)
    for k in range(1, slots):
        other = pltpu.roll(offset, k, 0)
        first = (other < offset) | ((other == offset) & (row >= k))
        colour = colour + jnp.where(first, 1, 0)
    colour = colour.astype(jnp.float32)

    def total(x):
        return jnp.sum(jnp.sum(x, axis=0, keepdims=True), axis=1, keepdims=True)

    for s in range(slots):
        hit = jnp.where(packing == (me[0] * slots + s).astype(jnp.float32), 1.0, 0.0)
        size = total(hit * lengths)
        reward = total(hit * rewards)
        same = jnp.where(groups == total(hit * groups), 1.0, 0.0)
        mean = total(same * rewards) / jnp.maximum(total(same), 1.0)
        advantage = (reward - mean).astype(jnp.bfloat16).astype(jnp.float32)
        factor[s : s + 1, :] = jnp.broadcast_to(-advantage * seq / size, (1, 128))
        colours[s] = total(hit * colour)[0, 0].astype(jnp.int32)
        length[s] = size[0, 0].astype(jnp.int32)


def plan(me, info, slots, dp, fsdp, seq):
    smem = pl.BlockSpec(memory_space=pltpu.SMEM)
    vmem = pl.BlockSpec(memory_space=pltpu.VMEM)
    return pl.pallas_call(
        functools.partial(plan_body, slots, dp, fsdp, seq),
        in_specs=[smem, vmem],
        out_specs=[smem, smem, vmem],
        out_shape=[
            jax.ShapeDtypeStruct((slots,), jnp.int32),
            jax.ShapeDtypeStruct((slots,), jnp.int32),
            jax.ShapeDtypeStruct((slots, 128), jnp.float32),
        ],
        cost_estimate=pl.CostEstimate(flops=1, bytes_accessed=1, transcendentals=0),
        name="plan_slots",
    )(me, info)


def stack_heads(ref, kh, group):
    cols = [ref[:, (kh * group + g) * HD : (kh * group + g + 1) * HD] for g in range(group)]
    return jnp.concatenate(cols, axis=0)


def probs_body(kv, group, slots, length, colours, factor, q, k, og, dv, turned, probs, held):
    s = pl.program_id(0)
    seq = q.shape[0]
    size = length[s]
    scale = factor[pl.ds(s, 1), :]
    key_pos = lax.broadcasted_iota(jnp.int32, (seq, group * seq), 0)
    query_pos = lax.rem(lax.broadcasted_iota(jnp.int32, (seq, group * seq), 1), seq)
    allowed = (key_pos <= query_pos) & (key_pos < size)
    live = query_pos < size
    shares = []
    for kh in range(kv):
        queries = stack_heads(q, kh, group)
        keys = k[:, kh * HD : (kh + 1) * HD]
        scores = lax.dot_general(
            keys, queries, (((1,), (1,)), ((), ())), preferred_element_type=jnp.float32
        ) / jnp.sqrt(jnp.float32(HD))
        masked = jnp.where(allowed, scores, -jnp.inf)
        top = jnp.max(masked, axis=0, keepdims=True)
        weights = jnp.where(allowed, jnp.exp(masked - top), 0.0)
        share = weights / jnp.sum(weights, axis=0, keepdims=True)
        share = jnp.where(live, share, 0.0)
        shares.append(share)
        share = share.astype(jnp.bfloat16)
        grads = stack_heads(og, kh, group)
        part = jnp.dot(share, grads, preferred_element_type=jnp.float32)
        part = (part * scale).astype(jnp.bfloat16)
        dv[:, kh * HD : (kh + 1) * HD] = part
        held[colours[s], :, kh * HD : (kh + 1) * HD] = part
    probs[0] = jnp.concatenate(shares, axis=0).T.astype(jnp.bfloat16)

    @pl.when(s == slots - 1)
    def _():
        turned[...] = held[...].reshape(slots * seq, kv * HD).T


def probs_and_dvalues(length, colours, factor, queries, keys, out_grad, slots):
    tokens, width = queries.shape
    seq = tokens // slots
    kv = keys.shape[1] // HD
    group = width // HD // kv
    return pl.pallas_call(
        functools.partial(probs_body, kv, group, slots),
        grid_spec=pltpu.PrefetchScalarGridSpec(
            num_scalar_prefetch=2,
            grid=(slots,),
            in_specs=[
                pl.BlockSpec((slots, 128), lambda s, n, c: (0, 0)),
                pl.BlockSpec((seq, width), lambda s, n, c: (s, 0)),
                pl.BlockSpec((seq, keys.shape[1]), lambda s, n, c: (s, 0)),
                pl.BlockSpec((seq, width), lambda s, n, c: (s, 0)),
            ],
            out_specs=[
                pl.BlockSpec((seq, keys.shape[1]), lambda s, n, c: (s, 0)),
                pl.BlockSpec((keys.shape[1], tokens), lambda s, n, c: (0, 0)),
                pl.BlockSpec((1, group * seq, kv * seq), lambda s, n, c: (s, 0, 0)),
            ],
            scratch_shapes=[pltpu.VMEM((slots, seq, keys.shape[1]), jnp.bfloat16)],
        ),
        out_shape=[
            jax.ShapeDtypeStruct((tokens, keys.shape[1]), jnp.bfloat16),
            jax.ShapeDtypeStruct((keys.shape[1], tokens), jnp.bfloat16),
            jax.ShapeDtypeStruct((slots, group * seq, kv * seq), jnp.bfloat16),
        ],
        compiler_params=params(),
        cost_estimate=pl.CostEstimate(flops=1, bytes_accessed=1, transcendentals=0),
        name="probs_dvalues",
    )(length, colours, factor, queries, keys, out_grad)


def values_body(steps, where, rows, *rest):
    weights, out, acc = rest[:4], rest[4], rest[5]
    step = pl.program_id(0)
    dp, _, _, _, seq, part = rows.shape
    lhs, rhs = [], []
    for n, w in enumerate(weights):
        x = rows[:, 0, lax.rem(where[4] + n // 2, 2), lax.rem(where[2] + n % 2, 2)]
        lhs.append(x.reshape(dp * seq, part))
        rhs.append(w[0])
    total = jnp.dot(
        jnp.concatenate(lhs, axis=1),
        jnp.concatenate(rhs, axis=0),
        preferred_element_type=jnp.float32,
    )

    @pl.when(step == 0)
    def _():
        acc[...] = total

    @pl.when(step > 0)
    def _():
        acc[...] += total

    @pl.when(step == steps - 1)
    def _():
        out[...] = acc[...].astype(out.dtype).reshape(out.shape)


def values_of(where, rows, weights):
    dp, around, cores, high, seq, part = rows.shape
    cols = weights[0].shape[2]
    return pl.pallas_call(
        functools.partial(values_body, around),
        grid_spec=pltpu.PrefetchScalarGridSpec(
            num_scalar_prefetch=1,
            grid=(around,),
            in_specs=[
                pl.BlockSpec(
                    (dp, 1, cores, high, seq, part),
                    lambda i, n: (0, lax.rem(n[3] - i + around, around), 0, 0, 0, 0),
                )
            ]
            + [pl.BlockSpec((1, part, cols), lambda i, n: (i, 0, 0))] * 4,
            out_specs=pl.BlockSpec((dp, seq, cols), lambda i, n: (0, 0, 0)),
            scratch_shapes=[pltpu.VMEM((dp * seq, cols), jnp.float32)],
        ),
        out_shape=jax.ShapeDtypeStruct((dp, seq, cols), jnp.bfloat16),
        compiler_params=params(),
        cost_estimate=pl.CostEstimate(flops=1, bytes_accessed=1, transcendentals=0),
        name="values",
    )(where, rows, *weights)


def grad_rows_body(where, dv, *rest):
    weights, outs = rest[:4], rest[4]
    part = weights[0].shape[1]
    half = pl.program_id(0)

    def write(first, second):
        for c, w in enumerate((first, second)):
            outs[:, c * part : (c + 1) * part] = lax.dot_general(
                dv[...], w[0], (((1,), (1,)), ((), ())), preferred_element_type=jnp.float32
            ).astype(outs.dtype)

    for h in range(2):
        for c in range(2):

            @pl.when((half == h) & (where[4] == c))
            def _(h=h, c=c):
                write(weights[2 * c + h], weights[2 * (1 - c) + h])


def grad_rows_of(where, dv, weights):
    tokens, cols = dv.shape
    around, part, _ = weights[0].shape
    last = around - 1
    near = pl.BlockSpec((1, part, cols), lambda h, i, n: (i * (1 - h) + last * h, 0, 0))
    far = pl.BlockSpec((1, part, cols), lambda h, i, n: (i * h, 0, 0))
    return pl.pallas_call(
        grad_rows_body,
        grid_spec=pltpu.PrefetchScalarGridSpec(
            num_scalar_prefetch=1,
            grid=(2, around),
            in_specs=[pl.BlockSpec((tokens, cols), lambda h, i, n: (0, 0)), near, far, near, far],
            out_specs=pl.BlockSpec(
                (tokens, 2 * part),
                lambda h, i, n: (
                    0,
                    lax.rem(n[2] + h, 2) * around + lax.rem(n[3] - i + around, around),
                ),
            ),
        ),
        out_shape=jax.ShapeDtypeStruct((tokens, 4 * around * part), jnp.bfloat16),
        compiler_params=params(),
        cost_estimate=pl.CostEstimate(flops=1, bytes_accessed=1, transcendentals=0),
        name="grad_rows",
    )(where, dv, *weights)


def attend_body(kv, group, levels, each, colours, where, probs, *rest):
    values, out, held = rest[:levels], rest[levels], rest[levels + 1]
    step = pl.program_id(0)
    _, seq, cols = values[0].shape

    @pl.when(step == 0)
    def _():
        for k in range(levels):
            held[2 * k : 2 * k + 2] = values[k][...]

    for e in range(each):
        colour = colours[step * each + e]
        away = lax.rem(where[1] - colour + 2 * levels, levels)
        other = lax.rem(lax.div(where[1], levels) + lax.div(colour, levels), 2)
        mine = held[2 * away + other]
        zero = jnp.zeros((seq, HD), mine.dtype)
        blocks = []
        for kh in range(kv):
            row = [zero] * kv
            row[kh] = mine[:, kh * HD : (kh + 1) * HD]
            blocks.append(jnp.concatenate(row, axis=1))
        heads = jnp.dot(
            probs[e], jnp.concatenate(blocks, axis=0), preferred_element_type=jnp.float32
        ).astype(out.dtype)
        for kh in range(kv):
            for g in range(group):
                h = kh * group + g
                out[e * seq : (e + 1) * seq, h * HD : (h + 1) * HD] = heads[
                    g * seq : (g + 1) * seq, kh * HD : (kh + 1) * HD
                ]


def attend(colours, where, probs, values):
    slots, span, keys = probs.shape
    _, seq, cols = values[0].shape
    kv = cols // HD
    group = span // seq
    width = kv * group * HD
    levels = len(values)
    each = 2
    return pl.pallas_call(
        functools.partial(attend_body, kv, group, levels, each),
        grid_spec=pltpu.PrefetchScalarGridSpec(
            num_scalar_prefetch=2,
            grid=(slots // each,),
            in_specs=[pl.BlockSpec((each, span, keys), lambda s, c, w: (s, 0, 0))]
            + [pl.BlockSpec((2, seq, cols), lambda s, c, w: (0, 0, 0))] * levels,
            out_specs=pl.BlockSpec((each * seq, width), lambda s, c, w: (s, 0)),
            scratch_shapes=[pltpu.VMEM((2 * levels, seq, cols), jnp.bfloat16)],
        ),
        out_shape=jax.ShapeDtypeStruct((slots * seq, width), jnp.bfloat16),
        compiler_params=params(SMALL),
        cost_estimate=pl.CostEstimate(flops=1, bytes_accessed=1, transcendentals=0),
        name="attend",
    )(colours, where, probs, *values)


def product_body(scale, where, rows, near, far, out):
    colours, around, _, _, seq, width = rows.shape
    lhs, rhs = [], []
    for k in range(around):
        for other, dv in enumerate((near, far)):
            x = rows[:, lax.rem(where[3] - k + around, around), lax.rem(where[4] + other, 2), 0]
            rhs.append(x.reshape(colours * seq, width))
            lhs.append(dv[k])
    part = jnp.dot(
        jnp.concatenate(lhs, axis=1),
        jnp.concatenate(rhs, axis=0),
        preferred_element_type=jnp.float32,
    )
    out[...] = (part * scale).T.astype(out.dtype)


def product(where, rows, near, far, scale, apart, dtype):
    colours, around, cores, high, seq, width = rows.shape
    _, cols, tokens = near.shape
    return pl.pallas_call(
        functools.partial(product_body, scale),
        grid_spec=pltpu.PrefetchScalarGridSpec(
            num_scalar_prefetch=1,
            grid=(1,),
            in_specs=[
                pl.BlockSpec(
                    (colours, around, cores, 1, seq, width),
                    lambda i, n: (0, 0, 0, lax.rem(n[2] + apart, high), 0, 0),
                )
            ]
            + [pl.BlockSpec((around, cols, tokens), lambda i, n: (0, 0, 0))] * 2,
            out_specs=pl.BlockSpec((width, cols), lambda i, n: (0, 0)),
        ),
        out_shape=jax.ShapeDtypeStruct((width, cols), dtype),
        compiler_params=params(SMALL),
        cost_estimate=pl.CostEstimate(flops=1, bytes_accessed=1, transcendentals=0),
        name="weight_product",
    )(where, rows, near, far)


def swap_rows(x, fsdp):
    return lax.ppermute(x, "fsdp", [(i, (i + fsdp // 2) % fsdp) for i in range(fsdp)])


def step_along(x, fsdp, step):
    half = fsdp // 2
    to = [(i, i // half * half + (i + 2 * step) % half) for i in range(fsdp)]
    return lax.ppermute(x, "fsdp", to)


def neighbours(x, fsdp):
    return step_along(x, fsdp, 1), step_along(x, fsdp, -1)


def opposite(back, front, fsdp):
    middle = back.shape[0] // 2
    return jnp.concatenate(
        [step_along(back[:middle], fsdp, 1), step_along(front[middle:], fsdp, -1)], axis=0
    )


def swap_cores(x, fsdp):
    return lax.ppermute(x, "fsdp", [(i, i ^ 1) for i in range(fsdp)])


def shards(
    rollout_rows, rewards, group_ids, lengths, packing, queries, keys, out_grad, value_weight
):
    slots, seq, width = rollout_rows.shape
    dp = lax.axis_size("dp")
    fsdp = lax.axis_size("fsdp")
    part = width // fsdp
    home = lax.axis_index("dp")
    place = lax.axis_index("fsdp")
    around = fsdp // 4
    where = jnp.stack(
        [home * fsdp + place, home, place // (2 * around), place // 2 % around, place % 2]
    ).astype(jnp.int32)
    info, order = prepare(packing, lengths, rewards, group_ids, dp, fsdp)
    info = lax.all_to_all(info, ("dp", "fsdp"), split_axis=0, concat_axis=0, tiled=True)
    rows = pack(order, rollout_rows, fsdp)
    across = swap_rows(value_weight, fsdp)
    back, front = neighbours(value_weight, fsdp)
    rows, info, across, back, front = lax.optimization_barrier(
        (rows, info, across, back, front)
    )
    rows = lax.all_to_all(
        rows.reshape(dp, fsdp * seq, part), "dp", split_axis=0, concat_axis=0, tiled=True
    )
    own = [value_weight, back, opposite(back, front, fsdp), front]
    across_back, across_front = neighbours(across, fsdp)
    length, colours, factor = plan(where, info, slots, dp, fsdp, seq)
    dvalues, turned, probs = probs_and_dvalues(
        length, colours, factor, queries, keys, out_grad, slots
    )
    dv_back, dv_front = neighbours(turned, fsdp)
    across_way = opposite(across_back, across_front, fsdp)
    across = [across, across_back, across_way, across_front]
    own, dvalues = lax.optimization_barrier((own, dvalues))
    own = jnp.stack(own)
    own_far = swap_cores(own, fsdp)
    across = jnp.stack(across)
    across_far = swap_cores(across, fsdp)
    weights = (own, across, own_far, across_far)
    near_dv = jnp.stack([turned, dv_back, opposite(dv_back, dv_front, fsdp), dv_front])
    far_dv = swap_cores(near_dv, fsdp)
    rows, dvalues, probs, weights, near_dv, far_dv = lax.optimization_barrier(
        (rows, dvalues, probs, weights, near_dv, far_dv)
    )
    rows = turn(order, rows)
    half = fsdp // 2
    groups = [
        [d * fsdp + h * half + i for d in range(dp) for i in range(half)] for h in range(2)
    ]
    sent = rows
    rows = lax.all_to_all(
        rows.reshape(dp * half, 2 * seq, part),
        ("dp", "fsdp"),
        split_axis=0,
        concat_axis=0,
        axis_index_groups=groups,
        tiled=True,
    ).reshape(dp, around, 2, 2, seq, part)
    grad_rows = grad_rows_of(where, dvalues, weights)
    sent, grad_rows = lax.optimization_barrier((sent, grad_rows))
    values = values_of(where, sent.reshape(dp, around, 2, 2, seq, part), weights)
    side, level = home // 4, home % 4
    keep = lax.dynamic_slice_in_dim(values, side * 4, 4, 0)
    give = lax.dynamic_slice_in_dim(values, (1 - side) * 4, 4, 0)
    got = lax.ppermute(give, "dp", [(i, (i + 4) % dp) for i in range(dp)])
    rows, got = lax.optimization_barrier((rows, got))
    both = [
        jnp.stack([lax.dynamic_index_in_dim(v, (level + k) % 4, 0, False) for v in (keep, got)])
        for k in range(4)
    ]
    held = [both[0]] + [
        lax.ppermute(both[k], "dp", [(i, i // 4 * 4 + (i + k) % 4) for i in range(dp)])
        for k in range(1, 4)
    ]
    given = product(where, rows, near_dv, far_dv, 1.0 / fsdp, 1, jnp.bfloat16)
    rows, given = lax.optimization_barrier((rows, given))
    given = swap_rows(given, fsdp)
    own = product(where, rows, near_dv, far_dv, 1.0 / fsdp, 0, jnp.float32)
    attn_out = attend(colours, where, probs, held)
    given, own, attn_out = lax.optimization_barrier((given, own, attn_out))
    grad_weight = (own + given.astype(jnp.float32)).astype(jnp.bfloat16)[None]
    return (attn_out, grad_rows, grad_weight)


def solution(mesh):
    in_specs = (
        P(("dp", "fsdp"), None, None),
        P(("dp", "fsdp")),
        P(("dp", "fsdp")),
        P(("dp", "fsdp")),
        P(("dp", "fsdp")),
        P(("dp", "fsdp"), None),
        P(("dp", "fsdp"), None),
        P(("dp", "fsdp"), None),
        P("fsdp", None),
    )
    out_specs = (P(("dp", "fsdp"), None), P(("dp", "fsdp"), None), P("dp", "fsdp", None))
    return jax.shard_map(shards, mesh=mesh, in_specs=in_specs, out_specs=out_specs, check_vma=False)
```

```python
import functools

import jax
import jax.numpy as jnp
from jax import lax
from jax.experimental import pallas as pl
from jax.experimental.pallas import tpu as pltpu
from jax.sharding import PartitionSpec as P

HD = 128
VMEM = 56 * 1024 * 1024
SMALL = 24 * 1024 * 1024


def params(limit=VMEM):
    return pltpu.CompilerParams(vmem_limit_bytes=limit)


def prepare_body(slots, dp, fsdp, packing, lengths, rewards, groups, info, order):
    lane = lax.broadcasted_iota(jnp.int32, info.shape, 1)
    told = jnp.zeros(info.shape, jnp.float32)
    for r in range(slots):
        told = jnp.where(lane == r, packing[r].astype(jnp.float32), told)
        told = jnp.where(lane == slots + r, lengths[r].astype(jnp.float32), told)
        told = jnp.where(lane == 2 * slots + r, rewards[r], told)
        told = jnp.where(lane == 3 * slots + r, groups[r].astype(jnp.float32), told)
    info[...] = told
    home = lax.axis_index("dp")
    offsets = [lax.rem(lax.div(packing[r], slots * fsdp) - home + dp, dp) for r in range(slots)]
    mine = jnp.int32(0)
    for r in range(slots):
        colour = jnp.int32(0)
        for k in range(slots):
            if k != r:
                first = offsets[k] <= offsets[r] if k < r else offsets[k] < offsets[r]
                colour = colour + jnp.where(first, 1, 0)
        order[r] = colour
        mine = mine + jnp.where(colour == home, offsets[r], 0)
    order[slots] = mine


def prepare(packing, lengths, rewards, groups, dp, fsdp):
    slots = packing.shape[0]
    smem = pl.BlockSpec(memory_space=pltpu.SMEM)
    return pl.pallas_call(
        functools.partial(prepare_body, slots, dp, fsdp),
        in_specs=[smem] * 4,
        out_specs=[pl.BlockSpec(memory_space=pltpu.VMEM), smem],
        out_shape=[
            jax.ShapeDtypeStruct((dp * fsdp, 4 * slots), jnp.float32),
            jax.ShapeDtypeStruct((slots + 1,), jnp.int32),
        ],
        name="prepare",
    )(packing, lengths, rewards, groups)


def pack_body(fsdp, order, rows, out, held, cut, arrive, leave):
    slots, _, width = rows.shape
    part = width // fsdp
    ins = [pltpu.make_async_copy(rows.at[r], held.at[r], arrive.at[r]) for r in range(slots)]
    outs = [pltpu.make_async_copy(cut.at[r], out.at[order[r]], leave.at[r]) for r in range(slots)]
    half = fsdp // 2
    for copy in ins:
        copy.start()
    for r in range(slots):
        ins[r].wait()
        for f in range(fsdp):
            cut[r, f % half * 2 + f // half] = held[r, :, f * part : (f + 1) * part]
        outs[r].start()
    for copy in outs:
        copy.wait()


def pack(order, rows, fsdp):
    slots, seq, width = rows.shape
    part = width // fsdp
    return pl.pallas_call(
        functools.partial(pack_body, fsdp),
        in_specs=[pl.BlockSpec(memory_space=pltpu.SMEM), pl.BlockSpec(memory_space=pl.ANY)],
        out_specs=pl.BlockSpec(memory_space=pl.ANY),
        out_shape=jax.ShapeDtypeStruct((slots, fsdp, seq, part), rows.dtype),
        scratch_shapes=[
            pltpu.VMEM((slots, seq, width), rows.dtype),
            pltpu.VMEM((slots, fsdp, seq, part), rows.dtype),
            pltpu.SemaphoreType.DMA((slots,)),
            pltpu.SemaphoreType.DMA((slots,)),
        ],
        compiler_params=params(),
        cost_estimate=pl.CostEstimate(
            flops=0, bytes_accessed=2 * rows.size * 2, transcendentals=0
        ),
        name="pack_rows",
    )(order, rows)


def turn_body(dp, slots, order, rows, out, held, arrive, leave):
    ins = [pltpu.make_async_copy(rows.at[p], held.at[p], arrive.at[p]) for p in range(dp)]
    outs = []
    for p in range(dp):
        dest = lax.rem(order[slots] + p, dp)
        outs.append(pltpu.make_async_copy(held.at[p], out.at[dest], leave.at[p]))
    for copy in ins:
        copy.start()
    for p in range(dp):
        ins[p].wait()
        outs[p].start()
    for copy in outs:
        copy.wait()


def turn(order, rows):
    dp = rows.shape[0]
    return pl.pallas_call(
        functools.partial(turn_body, dp, order.shape[0] - 1),
        in_specs=[pl.BlockSpec(memory_space=pltpu.SMEM), pl.BlockSpec(memory_space=pl.ANY)],
        out_specs=pl.BlockSpec(memory_space=pl.ANY),
        out_shape=jax.ShapeDtypeStruct(rows.shape, rows.dtype),
        scratch_shapes=[
            pltpu.VMEM(rows.shape, rows.dtype),
            pltpu.SemaphoreType.DMA((dp,)),
            pltpu.SemaphoreType.DMA((dp,)),
        ],
        compiler_params=params(),
        cost_estimate=pl.CostEstimate(
            flops=0, bytes_accessed=2 * rows.size * 2, transcendentals=0
        ),
        name="turn_rows",
    )(order, rows)


def plan_body(slots, dp, fsdp, seq, me, info, length, colours, factor):
    told = info[...].T
    packing = told[0:slots, :]
    lengths = told[slots : 2 * slots, :]
    rewards = told[2 * slots : 3 * slots, :]
    groups = told[3 * slots : 4 * slots, :]
    lane = lax.broadcasted_iota(jnp.int32, packing.shape, 1)
    row = lax.broadcasted_iota(jnp.int32, packing.shape, 0)
    target = lax.div(packing.astype(jnp.int32), slots * fsdp)

    offset = lax.rem(target - lax.div(lane, fsdp) + dp, dp)
    colour = jnp.zeros(packing.shape, jnp.int32)
    for k in range(1, slots):
        other = pltpu.roll(offset, k, 0)
        first = (other < offset) | ((other == offset) & (row >= k))
        colour = colour + jnp.where(first, 1, 0)
    colour = colour.astype(jnp.float32)

    def total(x):
        return jnp.sum(jnp.sum(x, axis=0, keepdims=True), axis=1, keepdims=True)

    for s in range(slots):
        hit = jnp.where(packing == (me[0] * slots + s).astype(jnp.float32), 1.0, 0.0)
        size = total(hit * lengths)
        reward = total(hit * rewards)
        same = jnp.where(groups == total(hit * groups), 1.0, 0.0)
        mean = total(same * rewards) / jnp.maximum(total(same), 1.0)
        advantage = (reward - mean).astype(jnp.bfloat16).astype(jnp.float32)
        factor[s : s + 1, :] = jnp.broadcast_to(-advantage * seq / size, (1, 128))
        colours[s] = total(hit * colour)[0, 0].astype(jnp.int32)
        length[s] = size[0, 0].astype(jnp.int32)


def plan(me, info, slots, dp, fsdp, seq):
    smem = pl.BlockSpec(memory_space=pltpu.SMEM)
    vmem = pl.BlockSpec(memory_space=pltpu.VMEM)
    return pl.pallas_call(
        functools.partial(plan_body, slots, dp, fsdp, seq),
        in_specs=[smem, vmem],
        out_specs=[smem, smem, vmem],
        out_shape=[
            jax.ShapeDtypeStruct((slots,), jnp.int32),
            jax.ShapeDtypeStruct((slots,), jnp.int32),
            jax.ShapeDtypeStruct((slots, 128), jnp.float32),
        ],
        cost_estimate=pl.CostEstimate(flops=1, bytes_accessed=1, transcendentals=0),
        name="plan_slots",
    )(me, info)


def stack_heads(ref, kh, group):
    cols = [ref[:, (kh * group + g) * HD : (kh * group + g + 1) * HD] for g in range(group)]
    return jnp.concatenate(cols, axis=0)


def probs_body(kv, group, slots, length, colours, factor, q, k, og, dv, turned, probs, held):
    s = pl.program_id(0)
    seq = q.shape[0]
    size = length[s]
    scale = factor[pl.ds(s, 1), :]
    key_pos = lax.broadcasted_iota(jnp.int32, (seq, group * seq), 0)
    query_pos = lax.rem(lax.broadcasted_iota(jnp.int32, (seq, group * seq), 1), seq)
    allowed = (key_pos <= query_pos) & (key_pos < size)
    live = query_pos < size
    shares = []
    for kh in range(kv):
        queries = stack_heads(q, kh, group)
        keys = k[:, kh * HD : (kh + 1) * HD]
        scores = lax.dot_general(
            keys, queries, (((1,), (1,)), ((), ())), preferred_element_type=jnp.float32
        ) / jnp.sqrt(jnp.float32(HD))
        masked = jnp.where(allowed, scores, -jnp.inf)
        top = jnp.max(masked, axis=0, keepdims=True)
        weights = jnp.where(allowed, jnp.exp(masked - top), 0.0)
        share = weights / jnp.sum(weights, axis=0, keepdims=True)
        share = jnp.where(live, share, 0.0)
        shares.append(share)
        share = share.astype(jnp.bfloat16)
        grads = stack_heads(og, kh, group)
        part = jnp.dot(share, grads, preferred_element_type=jnp.float32)
        part = (part * scale).astype(jnp.bfloat16)
        dv[:, kh * HD : (kh + 1) * HD] = part
        held[colours[s], :, kh * HD : (kh + 1) * HD] = part
    probs[0] = jnp.concatenate(shares, axis=0).T.astype(jnp.bfloat16)

    @pl.when(s == slots - 1)
    def _():
        turned[...] = held[...].reshape(slots * seq, kv * HD).T


def probs_and_dvalues(length, colours, factor, queries, keys, out_grad, slots):
    tokens, width = queries.shape
    seq = tokens // slots
    kv = keys.shape[1] // HD
    group = width // HD // kv
    return pl.pallas_call(
        functools.partial(probs_body, kv, group, slots),
        grid_spec=pltpu.PrefetchScalarGridSpec(
            num_scalar_prefetch=2,
            grid=(slots,),
            in_specs=[
                pl.BlockSpec((slots, 128), lambda s, n, c: (0, 0)),
                pl.BlockSpec((seq, width), lambda s, n, c: (s, 0)),
                pl.BlockSpec((seq, keys.shape[1]), lambda s, n, c: (s, 0)),
                pl.BlockSpec((seq, width), lambda s, n, c: (s, 0)),
            ],
            out_specs=[
                pl.BlockSpec((seq, keys.shape[1]), lambda s, n, c: (s, 0)),
                pl.BlockSpec((keys.shape[1], tokens), lambda s, n, c: (0, 0)),
                pl.BlockSpec((1, group * seq, kv * seq), lambda s, n, c: (s, 0, 0)),
            ],
            scratch_shapes=[pltpu.VMEM((slots, seq, keys.shape[1]), jnp.bfloat16)],
        ),
        out_shape=[
            jax.ShapeDtypeStruct((tokens, keys.shape[1]), jnp.bfloat16),
            jax.ShapeDtypeStruct((keys.shape[1], tokens), jnp.bfloat16),
            jax.ShapeDtypeStruct((slots, group * seq, kv * seq), jnp.bfloat16),
        ],
        compiler_params=params(),
        cost_estimate=pl.CostEstimate(flops=1, bytes_accessed=1, transcendentals=0),
        name="probs_dvalues",
    )(length, colours, factor, queries, keys, out_grad)


def values_body(steps, where, rows, *rest):
    weights, out, acc = rest[:4], rest[4], rest[5]
    step = pl.program_id(0)
    dp, _, _, _, seq, part = rows.shape
    lhs, rhs = [], []
    for n, w in enumerate(weights):
        x = rows[:, 0, lax.rem(where[4] + n // 2, 2), lax.rem(where[2] + n % 2, 2)]
        lhs.append(x.reshape(dp * seq, part))
        rhs.append(w[0])
    total = jnp.dot(
        jnp.concatenate(lhs, axis=1),
        jnp.concatenate(rhs, axis=0),
        preferred_element_type=jnp.float32,
    )

    @pl.when(step == 0)
    def _():
        acc[...] = total

    @pl.when(step > 0)
    def _():
        acc[...] += total

    @pl.when(step == steps - 1)
    def _():
        out[...] = acc[...].astype(out.dtype).reshape(out.shape)


def values_of(where, rows, weights):
    dp, around, cores, high, seq, part = rows.shape
    cols = weights[0].shape[2]
    return pl.pallas_call(
        functools.partial(values_body, around),
        grid_spec=pltpu.PrefetchScalarGridSpec(
            num_scalar_prefetch=1,
            grid=(around,),
            in_specs=[
                pl.BlockSpec(
                    (dp, 1, cores, high, seq, part),
                    lambda i, n: (0, lax.rem(n[3] - i + around, around), 0, 0, 0, 0),
                )
            ]
            + [pl.BlockSpec((1, part, cols), lambda i, n: (i, 0, 0))] * 4,
            out_specs=pl.BlockSpec((dp, seq, cols), lambda i, n: (0, 0, 0)),
            scratch_shapes=[pltpu.VMEM((dp * seq, cols), jnp.float32)],
        ),
        out_shape=jax.ShapeDtypeStruct((dp, seq, cols), jnp.bfloat16),
        compiler_params=params(),
        cost_estimate=pl.CostEstimate(flops=1, bytes_accessed=1, transcendentals=0),
        name="values",
    )(where, rows, *weights)


def grad_rows_body(where, dv, *rest):
    weights, outs = rest[:4], rest[4]
    part = weights[0].shape[1]
    half = pl.program_id(0)

    def write(first, second):
        for c, w in enumerate((first, second)):
            outs[:, c * part : (c + 1) * part] = lax.dot_general(
                dv[...], w[0], (((1,), (1,)), ((), ())), preferred_element_type=jnp.float32
            ).astype(outs.dtype)

    for h in range(2):
        for c in range(2):

            @pl.when((half == h) & (where[4] == c))
            def _(h=h, c=c):
                write(weights[2 * c + h], weights[2 * (1 - c) + h])


def grad_rows_of(where, dv, weights):
    tokens, cols = dv.shape
    around, part, _ = weights[0].shape
    last = around - 1
    near = pl.BlockSpec((1, part, cols), lambda h, i, n: (i * (1 - h) + last * h, 0, 0))
    far = pl.BlockSpec((1, part, cols), lambda h, i, n: (i * h, 0, 0))
    return pl.pallas_call(
        grad_rows_body,
        grid_spec=pltpu.PrefetchScalarGridSpec(
            num_scalar_prefetch=1,
            grid=(2, around),
            in_specs=[pl.BlockSpec((tokens, cols), lambda h, i, n: (0, 0)), near, far, near, far],
            out_specs=pl.BlockSpec(
                (tokens, 2 * part),
                lambda h, i, n: (
                    0,
                    lax.rem(n[2] + h, 2) * around + lax.rem(n[3] - i + around, around),
                ),
            ),
        ),
        out_shape=jax.ShapeDtypeStruct((tokens, 4 * around * part), jnp.bfloat16),
        compiler_params=params(),
        cost_estimate=pl.CostEstimate(flops=1, bytes_accessed=1, transcendentals=0),
        name="grad_rows",
    )(where, dv, *weights)


def attend_body(kv, group, levels, each, colours, where, probs, *rest):
    values, out, held = rest[:levels], rest[levels], rest[levels + 1]
    step = pl.program_id(0)
    _, seq, cols = values[0].shape

    @pl.when(step == 0)
    def _():
        for k in range(levels):
            held[2 * k : 2 * k + 2] = values[k][...]

    for e in range(each):
        colour = colours[step * each + e]
        away = lax.rem(where[1] - colour + 2 * levels, levels)
        other = lax.rem(lax.div(where[1], levels) + lax.div(colour, levels), 2)
        mine = held[2 * away + other]
        zero = jnp.zeros((seq, HD), mine.dtype)
        blocks = []
        for kh in range(kv):
            row = [zero] * kv
            row[kh] = mine[:, kh * HD : (kh + 1) * HD]
            blocks.append(jnp.concatenate(row, axis=1))
        heads = jnp.dot(
            probs[e], jnp.concatenate(blocks, axis=0), preferred_element_type=jnp.float32
        ).astype(out.dtype)
        for kh in range(kv):
            for g in range(group):
                h = kh * group + g
                out[e * seq : (e + 1) * seq, h * HD : (h + 1) * HD] = heads[
                    g * seq : (g + 1) * seq, kh * HD : (kh + 1) * HD
                ]


def attend(colours, where, probs, values):
    slots, span, keys = probs.shape
    _, seq, cols = values[0].shape
    kv = cols // HD
    group = span // seq
    width = kv * group * HD
    levels = len(values)
    each = 2
    return pl.pallas_call(
        functools.partial(attend_body, kv, group, levels, each),
        grid_spec=pltpu.PrefetchScalarGridSpec(
            num_scalar_prefetch=2,
            grid=(slots // each,),
            in_specs=[pl.BlockSpec((each, span, keys), lambda s, c, w: (s, 0, 0))]
            + [pl.BlockSpec((2, seq, cols), lambda s, c, w: (0, 0, 0))] * levels,
            out_specs=pl.BlockSpec((each * seq, width), lambda s, c, w: (s, 0)),
            scratch_shapes=[pltpu.VMEM((2 * levels, seq, cols), jnp.bfloat16)],
        ),
        out_shape=jax.ShapeDtypeStruct((slots * seq, width), jnp.bfloat16),
        compiler_params=params(SMALL),
        cost_estimate=pl.CostEstimate(flops=1, bytes_accessed=1, transcendentals=0),
        name="attend",
    )(colours, where, probs, *values)


def product_body(scale, where, rows, near, far, out):
    colours, around, _, _, seq, width = rows.shape
    lhs, rhs = [], []
    for k in range(around):
        for other, dv in enumerate((near, far)):
            x = rows[:, lax.rem(where[3] - k + around, around), lax.rem(where[4] + other, 2), 0]
            rhs.append(x.reshape(colours * seq, width))
            lhs.append(dv[k])
    part = jnp.dot(
        jnp.concatenate(lhs, axis=1),
        jnp.concatenate(rhs, axis=0),
        preferred_element_type=jnp.float32,
    )
    out[...] = (part * scale).T.astype(out.dtype)


def product(where, rows, near, far, scale, apart, dtype):
    colours, around, cores, high, seq, width = rows.shape
    _, cols, tokens = near.shape
    return pl.pallas_call(
        functools.partial(product_body, scale),
        grid_spec=pltpu.PrefetchScalarGridSpec(
            num_scalar_prefetch=1,
            grid=(1,),
            in_specs=[
                pl.BlockSpec(
                    (colours, around, cores, 1, seq, width),
                    lambda i, n: (0, 0, 0, lax.rem(n[2] + apart, high), 0, 0),
                )
            ]
            + [pl.BlockSpec((around, cols, tokens), lambda i, n: (0, 0, 0))] * 2,
            out_specs=pl.BlockSpec((width, cols), lambda i, n: (0, 0)),
        ),
        out_shape=jax.ShapeDtypeStruct((width, cols), dtype),
        compiler_params=params(SMALL),
        cost_estimate=pl.CostEstimate(flops=1, bytes_accessed=1, transcendentals=0),
        name="weight_product",
    )(where, rows, near, far)


def swap_rows(x, fsdp):
    return lax.ppermute(x, "fsdp", [(i, (i + fsdp // 2) % fsdp) for i in range(fsdp)])


def step_along(x, fsdp, step):
    half = fsdp // 2
    to = [(i, i // half * half + (i + 2 * step) % half) for i in range(fsdp)]
    return lax.ppermute(x, "fsdp", to)


def neighbours(x, fsdp):
    return step_along(x, fsdp, 1), step_along(x, fsdp, -1)


def opposite(back, front, fsdp):
    middle = back.shape[0] // 2
    return jnp.concatenate(
        [step_along(back[:middle], fsdp, 1), step_along(front[middle:], fsdp, -1)], axis=0
    )


def swap_cores(x, fsdp):
    return lax.ppermute(x, "fsdp", [(i, i ^ 1) for i in range(fsdp)])


def shards(
    rollout_rows, rewards, group_ids, lengths, packing, queries, keys, out_grad, value_weight
):
    slots, seq, width = rollout_rows.shape
    dp = lax.axis_size("dp")
    fsdp = lax.axis_size("fsdp")
    part = width // fsdp
    home = lax.axis_index("dp")
    place = lax.axis_index("fsdp")
    around = fsdp // 4
    where = jnp.stack(
        [home * fsdp + place, home, place // (2 * around), place // 2 % around, place % 2]
    ).astype(jnp.int32)
    info, order = prepare(packing, lengths, rewards, group_ids, dp, fsdp)
    info = lax.all_to_all(info, ("dp", "fsdp"), split_axis=0, concat_axis=0, tiled=True)
    rows = pack(order, rollout_rows, fsdp)
    across = swap_rows(value_weight, fsdp)
    back, front = neighbours(value_weight, fsdp)
    rows, info, across, back, front = lax.optimization_barrier(
        (rows, info, across, back, front)
    )
    rows = lax.all_to_all(
        rows.reshape(dp, fsdp * seq, part), "dp", split_axis=0, concat_axis=0, tiled=True
    )
    own = [value_weight, back, opposite(back, front, fsdp), front]
    across_back, across_front = neighbours(across, fsdp)
    length, colours, factor = plan(where, info, slots, dp, fsdp, seq)
    dvalues, turned, probs = probs_and_dvalues(
        length, colours, factor, queries, keys, out_grad, slots
    )
    dv_back, dv_front = neighbours(turned, fsdp)
    across_way = opposite(across_back, across_front, fsdp)
    across = [across, across_back, across_way, across_front]
    own, dvalues = lax.optimization_barrier((own, dvalues))
    own = jnp.stack(own)
    own_far = swap_cores(own, fsdp)
    across = jnp.stack(across)
    across_far = swap_cores(across, fsdp)
    weights = (own, across, own_far, across_far)
    near_dv = jnp.stack([turned, dv_back, opposite(dv_back, dv_front, fsdp), dv_front])
    far_dv = swap_cores(near_dv, fsdp)
    rows, dvalues, probs, weights, near_dv, far_dv = lax.optimization_barrier(
        (rows, dvalues, probs, weights, near_dv, far_dv)
    )
    rows = turn(order, rows)
    half = fsdp // 2
    groups = [
        [d * fsdp + h * half + i for d in range(dp) for i in range(half)] for h in range(2)
    ]
    sent = rows
    rows = lax.all_to_all(
        rows.reshape(dp * half, 2 * seq, part),
        ("dp", "fsdp"),
        split_axis=0,
        concat_axis=0,
        axis_index_groups=groups,
        tiled=True,
    ).reshape(dp, around, 2, 2, seq, part)
    values = values_of(where, sent.reshape(dp, around, 2, 2, seq, part), weights)
    side, level = home // 4, home % 4
    keep = lax.dynamic_slice_in_dim(values, side * 4, 4, 0)
    give = lax.dynamic_slice_in_dim(values, (1 - side) * 4, 4, 0)
    got = lax.ppermute(give, "dp", [(i, (i + 4) % dp) for i in range(dp)])
    dvalues, values = lax.optimization_barrier((dvalues, values))
    grad_rows = grad_rows_of(where, dvalues, weights)
    rows, got, grad_rows = lax.optimization_barrier((rows, got, grad_rows))
    both = [
        jnp.stack([lax.dynamic_index_in_dim(v, (level + k) % 4, 0, False) for v in (keep, got)])
        for k in range(4)
    ]
    held = [both[0]] + [
        lax.ppermute(both[k], "dp", [(i, i // 4 * 4 + (i + k) % 4) for i in range(dp)])
        for k in range(1, 4)
    ]
    given = product(where, rows, near_dv, far_dv, 1.0 / fsdp, 1, jnp.bfloat16)
    rows, given = lax.optimization_barrier((rows, given))
    given = swap_rows(given, fsdp)
    own = product(where, rows, near_dv, far_dv, 1.0 / fsdp, 0, jnp.float32)
    attn_out = attend(colours, where, probs, held)
    given, own, attn_out = lax.optimization_barrier((given, own, attn_out))
    grad_weight = (own + given.astype(jnp.float32)).astype(jnp.bfloat16)[None]
    return (attn_out, grad_rows, grad_weight)


def solution(mesh):
    in_specs = (
        P(("dp", "fsdp"), None, None),
        P(("dp", "fsdp")),
        P(("dp", "fsdp")),
        P(("dp", "fsdp")),
        P(("dp", "fsdp")),
        P(("dp", "fsdp"), None),
        P(("dp", "fsdp"), None),
        P(("dp", "fsdp"), None),
        P("fsdp", None),
    )
    out_specs = (P(("dp", "fsdp"), None), P(("dp", "fsdp"), None), P("dp", "fsdp", None))
    return jax.shard_map(shards, mesh=mesh, in_specs=in_specs, out_specs=out_specs, check_vma=False)
```

```python
import functools

import jax
import jax.numpy as jnp
from jax import lax
from jax.experimental import pallas as pl
from jax.experimental.pallas import tpu as pltpu
from jax.sharding import PartitionSpec as P

HD = 128
VMEM = 56 * 1024 * 1024
SMALL = 24 * 1024 * 1024


def params(limit=VMEM):
    return pltpu.CompilerParams(vmem_limit_bytes=limit)


def prepare_body(slots, dp, fsdp, packing, lengths, rewards, groups, info, order):
    lane = lax.broadcasted_iota(jnp.int32, info.shape, 1)
    told = jnp.zeros(info.shape, jnp.float32)
    for r in range(slots):
        told = jnp.where(lane == r, packing[r].astype(jnp.float32), told)
        told = jnp.where(lane == slots + r, lengths[r].astype(jnp.float32), told)
        told = jnp.where(lane == 2 * slots + r, rewards[r], told)
        told = jnp.where(lane == 3 * slots + r, groups[r].astype(jnp.float32), told)
    info[...] = told
    home = lax.axis_index("dp")
    offsets = [lax.rem(lax.div(packing[r], slots * fsdp) - home + dp, dp) for r in range(slots)]
    mine = jnp.int32(0)
    for r in range(slots):
        colour = jnp.int32(0)
        for k in range(slots):
            if k != r:
                first = offsets[k] <= offsets[r] if k < r else offsets[k] < offsets[r]
                colour = colour + jnp.where(first, 1, 0)
        order[r] = colour
        mine = mine + jnp.where(colour == home, offsets[r], 0)
    order[slots] = mine


def prepare(packing, lengths, rewards, groups, dp, fsdp):
    slots = packing.shape[0]
    smem = pl.BlockSpec(memory_space=pltpu.SMEM)
    return pl.pallas_call(
        functools.partial(prepare_body, slots, dp, fsdp),
        in_specs=[smem] * 4,
        out_specs=[pl.BlockSpec(memory_space=pltpu.VMEM), smem],
        out_shape=[
            jax.ShapeDtypeStruct((dp * fsdp, 4 * slots), jnp.float32),
            jax.ShapeDtypeStruct((slots + 1,), jnp.int32),
        ],
        name="prepare",
    )(packing, lengths, rewards, groups)


def pack_body(fsdp, order, rows, out, held, cut, arrive, leave):
    slots, _, width = rows.shape
    part = width // fsdp
    ins = [pltpu.make_async_copy(rows.at[r], held.at[r], arrive.at[r]) for r in range(slots)]
    outs = [pltpu.make_async_copy(cut.at[r], out.at[order[r]], leave.at[r]) for r in range(slots)]
    half = fsdp // 2
    for copy in ins:
        copy.start()
    for r in range(slots):
        ins[r].wait()
        for f in range(fsdp):
            cut[r, f % half * 2 + f // half] = held[r, :, f * part : (f + 1) * part]
        outs[r].start()
    for copy in outs:
        copy.wait()


def pack(order, rows, fsdp):
    slots, seq, width = rows.shape
    part = width // fsdp
    return pl.pallas_call(
        functools.partial(pack_body, fsdp),
        in_specs=[pl.BlockSpec(memory_space=pltpu.SMEM), pl.BlockSpec(memory_space=pl.ANY)],
        out_specs=pl.BlockSpec(memory_space=pl.ANY),
        out_shape=jax.ShapeDtypeStruct((slots, fsdp, seq, part), rows.dtype),
        scratch_shapes=[
            pltpu.VMEM((slots, seq, width), rows.dtype),
            pltpu.VMEM((slots, fsdp, seq, part), rows.dtype),
            pltpu.SemaphoreType.DMA((slots,)),
            pltpu.SemaphoreType.DMA((slots,)),
        ],
        compiler_params=params(),
        cost_estimate=pl.CostEstimate(
            flops=0, bytes_accessed=2 * rows.size * 2, transcendentals=0
        ),
        name="pack_rows",
    )(order, rows)


def turn_body(dp, slots, order, rows, out, held, arrive, leave):
    ins = [pltpu.make_async_copy(rows.at[p], held.at[p], arrive.at[p]) for p in range(dp)]
    outs = []
    for p in range(dp):
        dest = lax.rem(order[slots] + p, dp)
        outs.append(pltpu.make_async_copy(held.at[p], out.at[dest], leave.at[p]))
    for copy in ins:
        copy.start()
    for p in range(dp):
        ins[p].wait()
        outs[p].start()
    for copy in outs:
        copy.wait()


def turn(order, rows):
    dp = rows.shape[0]
    return pl.pallas_call(
        functools.partial(turn_body, dp, order.shape[0] - 1),
        in_specs=[pl.BlockSpec(memory_space=pltpu.SMEM), pl.BlockSpec(memory_space=pl.ANY)],
        out_specs=pl.BlockSpec(memory_space=pl.ANY),
        out_shape=jax.ShapeDtypeStruct(rows.shape, rows.dtype),
        scratch_shapes=[
            pltpu.VMEM(rows.shape, rows.dtype),
            pltpu.SemaphoreType.DMA((dp,)),
            pltpu.SemaphoreType.DMA((dp,)),
        ],
        compiler_params=params(),
        cost_estimate=pl.CostEstimate(
            flops=0, bytes_accessed=2 * rows.size * 2, transcendentals=0
        ),
        name="turn_rows",
    )(order, rows)


def plan_body(slots, dp, fsdp, seq, me, info, length, colours, factor):
    told = info[...].T
    packing = told[0:slots, :]
    lengths = told[slots : 2 * slots, :]
    rewards = told[2 * slots : 3 * slots, :]
    groups = told[3 * slots : 4 * slots, :]
    lane = lax.broadcasted_iota(jnp.int32, packing.shape, 1)
    row = lax.broadcasted_iota(jnp.int32, packing.shape, 0)
    target = lax.div(packing.astype(jnp.int32), slots * fsdp)

    offset = lax.rem(target - lax.div(lane, fsdp) + dp, dp)
    colour = jnp.zeros(packing.shape, jnp.int32)
    for k in range(1, slots):
        other = pltpu.roll(offset, k, 0)
        first = (other < offset) | ((other == offset) & (row >= k))
        colour = colour + jnp.where(first, 1, 0)
    colour = colour.astype(jnp.float32)

    def total(x):
        return jnp.sum(jnp.sum(x, axis=0, keepdims=True), axis=1, keepdims=True)

    for s in range(slots):
        hit = jnp.where(packing == (me[0] * slots + s).astype(jnp.float32), 1.0, 0.0)
        size = total(hit * lengths)
        reward = total(hit * rewards)
        same = jnp.where(groups == total(hit * groups), 1.0, 0.0)
        mean = total(same * rewards) / jnp.maximum(total(same), 1.0)
        advantage = (reward - mean).astype(jnp.bfloat16).astype(jnp.float32)
        factor[s : s + 1, :] = jnp.broadcast_to(-advantage * seq / size, (1, 128))
        colours[s] = total(hit * colour)[0, 0].astype(jnp.int32)
        length[s] = size[0, 0].astype(jnp.int32)


def plan(me, info, slots, dp, fsdp, seq):
    smem = pl.BlockSpec(memory_space=pltpu.SMEM)
    vmem = pl.BlockSpec(memory_space=pltpu.VMEM)
    return pl.pallas_call(
        functools.partial(plan_body, slots, dp, fsdp, seq),
        in_specs=[smem, vmem],
        out_specs=[smem, smem, vmem],
        out_shape=[
            jax.ShapeDtypeStruct((slots,), jnp.int32),
            jax.ShapeDtypeStruct((slots,), jnp.int32),
            jax.ShapeDtypeStruct((slots, 128), jnp.float32),
        ],
        cost_estimate=pl.CostEstimate(flops=1, bytes_accessed=1, transcendentals=0),
        name="plan_slots",
    )(me, info)


def stack_heads(ref, kh, group):
    cols = [ref[:, (kh * group + g) * HD : (kh * group + g + 1) * HD] for g in range(group)]
    return jnp.concatenate(cols, axis=0)


def probs_body(kv, group, slots, length, colours, factor, q, k, og, dv, turned, probs, held):
    s = pl.program_id(0)
    seq = q.shape[0]
    size = length[s]
    scale = factor[pl.ds(s, 1), :]
    key_pos = lax.broadcasted_iota(jnp.int32, (seq, group * seq), 0)
    query_pos = lax.rem(lax.broadcasted_iota(jnp.int32, (seq, group * seq), 1), seq)
    allowed = (key_pos <= query_pos) & (key_pos < size)
    live = query_pos < size
    shares = []
    for kh in range(kv):
        queries = stack_heads(q, kh, group)
        keys = k[:, kh * HD : (kh + 1) * HD]
        scores = lax.dot_general(
            keys, queries, (((1,), (1,)), ((), ())), preferred_element_type=jnp.float32
        ) / jnp.sqrt(jnp.float32(HD))
        masked = jnp.where(allowed, scores, -jnp.inf)
        top = jnp.max(masked, axis=0, keepdims=True)
        weights = jnp.where(allowed, jnp.exp(masked - top), 0.0)
        share = weights / jnp.sum(weights, axis=0, keepdims=True)
        share = jnp.where(live, share, 0.0)
        shares.append(share)
        share = share.astype(jnp.bfloat16)
        grads = stack_heads(og, kh, group)
        part = jnp.dot(share, grads, preferred_element_type=jnp.float32)
        part = (part * scale).astype(jnp.bfloat16)
        dv[:, kh * HD : (kh + 1) * HD] = part
        held[colours[s], :, kh * HD : (kh + 1) * HD] = part
    probs[0] = jnp.concatenate(shares, axis=0).T.astype(jnp.bfloat16)

    @pl.when(s == slots - 1)
    def _():
        turned[...] = held[...].reshape(slots * seq, kv * HD).T


def probs_and_dvalues(length, colours, factor, queries, keys, out_grad, slots):
    tokens, width = queries.shape
    seq = tokens // slots
    kv = keys.shape[1] // HD
    group = width // HD // kv
    return pl.pallas_call(
        functools.partial(probs_body, kv, group, slots),
        grid_spec=pltpu.PrefetchScalarGridSpec(
            num_scalar_prefetch=2,
            grid=(slots,),
            in_specs=[
                pl.BlockSpec((slots, 128), lambda s, n, c: (0, 0)),
                pl.BlockSpec((seq, width), lambda s, n, c: (s, 0)),
                pl.BlockSpec((seq, keys.shape[1]), lambda s, n, c: (s, 0)),
                pl.BlockSpec((seq, width), lambda s, n, c: (s, 0)),
            ],
            out_specs=[
                pl.BlockSpec((seq, keys.shape[1]), lambda s, n, c: (s, 0)),
                pl.BlockSpec((keys.shape[1], tokens), lambda s, n, c: (0, 0)),
                pl.BlockSpec((1, group * seq, kv * seq), lambda s, n, c: (s, 0, 0)),
            ],
            scratch_shapes=[pltpu.VMEM((slots, seq, keys.shape[1]), jnp.bfloat16)],
        ),
        out_shape=[
            jax.ShapeDtypeStruct((tokens, keys.shape[1]), jnp.bfloat16),
            jax.ShapeDtypeStruct((keys.shape[1], tokens), jnp.bfloat16),
            jax.ShapeDtypeStruct((slots, group * seq, kv * seq), jnp.bfloat16),
        ],
        compiler_params=params(),
        cost_estimate=pl.CostEstimate(flops=1, bytes_accessed=1, transcendentals=0),
        name="probs_dvalues",
    )(length, colours, factor, queries, keys, out_grad)


def values_body(steps, where, rows, *rest):
    weights, out, acc = rest[:4], rest[4], rest[5]
    step = pl.program_id(0)
    dp, _, _, _, seq, part = rows.shape
    lhs, rhs = [], []
    for n, w in enumerate(weights):
        x = rows[:, 0, lax.rem(where[4] + n // 2, 2), lax.rem(where[2] + n % 2, 2)]
        lhs.append(x.reshape(dp * seq, part))
        rhs.append(w[0])
    total = jnp.dot(
        jnp.concatenate(lhs, axis=1),
        jnp.concatenate(rhs, axis=0),
        preferred_element_type=jnp.float32,
    )

    @pl.when(step == 0)
    def _():
        acc[...] = total

    @pl.when(step > 0)
    def _():
        acc[...] += total

    @pl.when(step == steps - 1)
    def _():
        out[...] = acc[...].astype(out.dtype).reshape(out.shape)


def values_of(where, rows, weights):
    dp, around, cores, high, seq, part = rows.shape
    cols = weights[0].shape[2]
    return pl.pallas_call(
        functools.partial(values_body, around),
        grid_spec=pltpu.PrefetchScalarGridSpec(
            num_scalar_prefetch=1,
            grid=(around,),
            in_specs=[
                pl.BlockSpec(
                    (dp, 1, cores, high, seq, part),
                    lambda i, n: (0, lax.rem(n[3] - i + around, around), 0, 0, 0, 0),
                )
            ]
            + [pl.BlockSpec((1, part, cols), lambda i, n: (i, 0, 0))] * 4,
            out_specs=pl.BlockSpec((dp, seq, cols), lambda i, n: (0, 0, 0)),
            scratch_shapes=[pltpu.VMEM((dp * seq, cols), jnp.float32)],
        ),
        out_shape=jax.ShapeDtypeStruct((dp, seq, cols), jnp.bfloat16),
        compiler_params=params(),
        cost_estimate=pl.CostEstimate(flops=1, bytes_accessed=1, transcendentals=0),
        name="values",
    )(where, rows, *weights)


def grad_rows_body(where, dv, *rest):
    weights, outs = rest[:4], rest[4]
    part = weights[0].shape[1]
    half = pl.program_id(0)

    def write(first, second):
        for c, w in enumerate((first, second)):
            outs[:, c * part : (c + 1) * part] = lax.dot_general(
                dv[...], w[0], (((1,), (1,)), ((), ())), preferred_element_type=jnp.float32
            ).astype(outs.dtype)

    for h in range(2):
        for c in range(2):

            @pl.when((half == h) & (where[4] == c))
            def _(h=h, c=c):
                write(weights[2 * c + h], weights[2 * (1 - c) + h])


def grad_rows_of(where, dv, weights):
    tokens, cols = dv.shape
    around, part, _ = weights[0].shape
    last = around - 1
    near = pl.BlockSpec((1, part, cols), lambda h, i, n: (i * (1 - h) + last * h, 0, 0))
    far = pl.BlockSpec((1, part, cols), lambda h, i, n: (i * h, 0, 0))
    return pl.pallas_call(
        grad_rows_body,
        grid_spec=pltpu.PrefetchScalarGridSpec(
            num_scalar_prefetch=1,
            grid=(2, around),
            in_specs=[pl.BlockSpec((tokens, cols), lambda h, i, n: (0, 0)), near, far, near, far],
            out_specs=pl.BlockSpec(
                (tokens, 2 * part),
                lambda h, i, n: (
                    0,
                    lax.rem(n[2] + h, 2) * around + lax.rem(n[3] - i + around, around),
                ),
            ),
        ),
        out_shape=jax.ShapeDtypeStruct((tokens, 4 * around * part), jnp.bfloat16),
        compiler_params=params(),
        cost_estimate=pl.CostEstimate(flops=1, bytes_accessed=1, transcendentals=0),
        name="grad_rows",
    )(where, dv, *weights)


def attend_body(kv, group, levels, each, colours, where, probs, *rest):
    values, out, held = rest[:levels], rest[levels], rest[levels + 1]
    step = pl.program_id(0)
    _, seq, cols = values[0].shape

    @pl.when(step == 0)
    def _():
        for k in range(levels):
            held[2 * k : 2 * k + 2] = values[k][...]

    for e in range(each):
        colour = colours[step * each + e]
        away = lax.rem(where[1] - colour + 2 * levels, levels)
        other = lax.rem(lax.div(where[1], levels) + lax.div(colour, levels), 2)
        mine = held[2 * away + other]
        zero = jnp.zeros((seq, HD), mine.dtype)
        blocks = []
        for kh in range(kv):
            row = [zero] * kv
            row[kh] = mine[:, kh * HD : (kh + 1) * HD]
            blocks.append(jnp.concatenate(row, axis=1))
        heads = jnp.dot(
            probs[e], jnp.concatenate(blocks, axis=0), preferred_element_type=jnp.float32
        ).astype(out.dtype)
        for kh in range(kv):
            for g in range(group):
                h = kh * group + g
                out[e * seq : (e + 1) * seq, h * HD : (h + 1) * HD] = heads[
                    g * seq : (g + 1) * seq, kh * HD : (kh + 1) * HD
                ]


def attend(colours, where, probs, values):
    slots, span, keys = probs.shape
    _, seq, cols = values[0].shape
    kv = cols // HD
    group = span // seq
    width = kv * group * HD
    levels = len(values)
    each = 4
    return pl.pallas_call(
        functools.partial(attend_body, kv, group, levels, each),
        grid_spec=pltpu.PrefetchScalarGridSpec(
            num_scalar_prefetch=2,
            grid=(slots // each,),
            in_specs=[pl.BlockSpec((each, span, keys), lambda s, c, w: (s, 0, 0))]
            + [pl.BlockSpec((2, seq, cols), lambda s, c, w: (0, 0, 0))] * levels,
            out_specs=pl.BlockSpec((each * seq, width), lambda s, c, w: (s, 0)),
            scratch_shapes=[pltpu.VMEM((2 * levels, seq, cols), jnp.bfloat16)],
        ),
        out_shape=jax.ShapeDtypeStruct((slots * seq, width), jnp.bfloat16),
        compiler_params=params(SMALL),
        cost_estimate=pl.CostEstimate(flops=1, bytes_accessed=1, transcendentals=0),
        name="attend",
    )(colours, where, probs, *values)


def product_body(scale, where, rows, near, far, out):
    colours, around, _, _, seq, width = rows.shape
    lhs, rhs = [], []
    for k in range(around):
        for other, dv in enumerate((near, far)):
            x = rows[:, lax.rem(where[3] - k + around, around), lax.rem(where[4] + other, 2), 0]
            rhs.append(x.reshape(colours * seq, width))
            lhs.append(dv[k])
    part = jnp.dot(
        jnp.concatenate(lhs, axis=1),
        jnp.concatenate(rhs, axis=0),
        preferred_element_type=jnp.float32,
    )
    out[...] = (part * scale).T.astype(out.dtype)


def product(where, rows, near, far, scale, apart, dtype):
    colours, around, cores, high, seq, width = rows.shape
    _, cols, tokens = near.shape
    return pl.pallas_call(
        functools.partial(product_body, scale),
        grid_spec=pltpu.PrefetchScalarGridSpec(
            num_scalar_prefetch=1,
            grid=(1,),
            in_specs=[
                pl.BlockSpec(
                    (colours, around, cores, 1, seq, width),
                    lambda i, n: (0, 0, 0, lax.rem(n[2] + apart, high), 0, 0),
                )
            ]
            + [pl.BlockSpec((around, cols, tokens), lambda i, n: (0, 0, 0))] * 2,
            out_specs=pl.BlockSpec((width, cols), lambda i, n: (0, 0)),
        ),
        out_shape=jax.ShapeDtypeStruct((width, cols), dtype),
        compiler_params=params(SMALL),
        cost_estimate=pl.CostEstimate(flops=1, bytes_accessed=1, transcendentals=0),
        name="weight_product",
    )(where, rows, near, far)


def swap_rows(x, fsdp):
    return lax.ppermute(x, "fsdp", [(i, (i + fsdp // 2) % fsdp) for i in range(fsdp)])


def step_along(x, fsdp, step):
    half = fsdp // 2
    to = [(i, i // half * half + (i + 2 * step) % half) for i in range(fsdp)]
    return lax.ppermute(x, "fsdp", to)


def neighbours(x, fsdp):
    return step_along(x, fsdp, 1), step_along(x, fsdp, -1)


def opposite(back, front, fsdp):
    middle = back.shape[0] // 2
    return jnp.concatenate(
        [step_along(back[:middle], fsdp, 1), step_along(front[middle:], fsdp, -1)], axis=0
    )


def swap_cores(x, fsdp):
    return lax.ppermute(x, "fsdp", [(i, i ^ 1) for i in range(fsdp)])


def shards(
    rollout_rows, rewards, group_ids, lengths, packing, queries, keys, out_grad, value_weight
):
    slots, seq, width = rollout_rows.shape
    dp = lax.axis_size("dp")
    fsdp = lax.axis_size("fsdp")
    part = width // fsdp
    home = lax.axis_index("dp")
    place = lax.axis_index("fsdp")
    around = fsdp // 4
    where = jnp.stack(
        [home * fsdp + place, home, place // (2 * around), place // 2 % around, place % 2]
    ).astype(jnp.int32)
    info, order = prepare(packing, lengths, rewards, group_ids, dp, fsdp)
    info = lax.all_to_all(info, ("dp", "fsdp"), split_axis=0, concat_axis=0, tiled=True)
    rows = pack(order, rollout_rows, fsdp)
    across = swap_rows(value_weight, fsdp)
    back, front = neighbours(value_weight, fsdp)
    rows, info, across, back, front = lax.optimization_barrier(
        (rows, info, across, back, front)
    )
    rows = lax.all_to_all(
        rows.reshape(dp, fsdp * seq, part), "dp", split_axis=0, concat_axis=0, tiled=True
    )
    own = [value_weight, back, opposite(back, front, fsdp), front]
    across_back, across_front = neighbours(across, fsdp)
    length, colours, factor = plan(where, info, slots, dp, fsdp, seq)
    dvalues, turned, probs = probs_and_dvalues(
        length, colours, factor, queries, keys, out_grad, slots
    )
    dv_back, dv_front = neighbours(turned, fsdp)
    across_way = opposite(across_back, across_front, fsdp)
    across = [across, across_back, across_way, across_front]
    own, dvalues = lax.optimization_barrier((own, dvalues))
    own = jnp.stack(own)
    own_far = swap_cores(own, fsdp)
    across = jnp.stack(across)
    across_far = swap_cores(across, fsdp)
    weights = (own, across, own_far, across_far)
    near_dv = jnp.stack([turned, dv_back, opposite(dv_back, dv_front, fsdp), dv_front])
    far_dv = swap_cores(near_dv, fsdp)
    rows, dvalues, probs, weights, near_dv, far_dv = lax.optimization_barrier(
        (rows, dvalues, probs, weights, near_dv, far_dv)
    )
    rows = turn(order, rows)
    half = fsdp // 2
    groups = [
        [d * fsdp + h * half + i for d in range(dp) for i in range(half)] for h in range(2)
    ]
    sent = rows
    rows = lax.all_to_all(
        rows.reshape(dp * half, 2 * seq, part),
        ("dp", "fsdp"),
        split_axis=0,
        concat_axis=0,
        axis_index_groups=groups,
        tiled=True,
    ).reshape(dp, around, 2, 2, seq, part)
    values = values_of(where, sent.reshape(dp, around, 2, 2, seq, part), weights)
    side, level = home // 4, home % 4
    keep = lax.dynamic_slice_in_dim(values, side * 4, 4, 0)
    give = lax.dynamic_slice_in_dim(values, (1 - side) * 4, 4, 0)
    got = lax.ppermute(give, "dp", [(i, (i + 4) % dp) for i in range(dp)])
    dvalues, values = lax.optimization_barrier((dvalues, values))
    grad_rows = grad_rows_of(where, dvalues, weights)
    rows, got, grad_rows = lax.optimization_barrier((rows, got, grad_rows))
    both = [
        jnp.stack([lax.dynamic_index_in_dim(v, (level + k) % 4, 0, False) for v in (keep, got)])
        for k in range(4)
    ]
    held = [both[0]] + [
        lax.ppermute(both[k], "dp", [(i, i // 4 * 4 + (i + k) % 4) for i in range(dp)])
        for k in range(1, 4)
    ]
    given = product(where, rows, near_dv, far_dv, 1.0 / fsdp, 1, jnp.bfloat16)
    rows, given = lax.optimization_barrier((rows, given))
    given = swap_rows(given, fsdp)
    own = product(where, rows, near_dv, far_dv, 1.0 / fsdp, 0, jnp.float32)
    attn_out = attend(colours, where, probs, held)
    given, own, attn_out = lax.optimization_barrier((given, own, attn_out))
    grad_weight = (own + given.astype(jnp.float32)).astype(jnp.bfloat16)[None]
    return (attn_out, grad_rows, grad_weight)


def solution(mesh):
    in_specs = (
        P(("dp", "fsdp"), None, None),
        P(("dp", "fsdp")),
        P(("dp", "fsdp")),
        P(("dp", "fsdp")),
        P(("dp", "fsdp")),
        P(("dp", "fsdp"), None),
        P(("dp", "fsdp"), None),
        P(("dp", "fsdp"), None),
        P("fsdp", None),
    )
    out_specs = (P(("dp", "fsdp"), None), P(("dp", "fsdp"), None), P("dp", "fsdp", None))
    return jax.shard_map(shards, mesh=mesh, in_specs=in_specs, out_specs=out_specs, check_vma=False)
```
